32 devices in a mesh: sect: 2 (over x), grp: 16 (over z, y, core), tp: 1.
Axes of the slice: x: 2, y: 2, z: 4, core: 2. Of those that a mesh axis runs over, the one named last changes fastest.
Arguments:
- queries: bfloat16 [512, 128, 576], P('grp', ('sect', 'tp')), may hold values from -400 to 400, as said below
- latent_cache: bfloat16 [512, 128, 576], P('grp'), may hold values from -6 to 6, as said below
- cache_len: int32 [512], P('grp'), may hold values from 1 to 128, 32768 in all
- value_up: bfloat16 [128, 512, 128], P(('sect', 'tp')), may hold values from -0.25 to 0.25
- out_proj: bfloat16 [16384, 7168], P(('sect', 'tp'), 'grp'), may hold values from -0.046875 to 0.046875
- residual: bfloat16 [512, 7168], P(None, 'grp'), may hold values from -3 to 3
- w_gate: bfloat16 [16, 7168, 2048], P('grp', None, ('sect', 'tp')), may hold values from -0.0625 to 0.0625
- w_up: bfloat16 [16, 7168, 2048], P('grp', None, ('sect', 'tp')), may hold values from -0.0625 to 0.0625
- w_down: bfloat16 [16, 2048, 7168], P('grp', ('sect', 'tp')), may hold values from -0.1875 to 0.1875
- route_ids: int32 [512, 8], replicated, may hold values from 0 to 15, all different within a row; in each aligned block of 512 rows (0 to 511, 512 to 1023, ...) at most 384 rows name the same one
- route_weights: float32 [512, 8], replicated, may hold values from 0.1 to 0.6
Outputs:
- layer_out: bfloat16 [512, 7168], P(('sect', 'tp'), 'grp')
The draws below stay inside these ranges and needn't reach their ends.
Inputs may be any that keep to these rules, and one draw needn't show every extreme that they name: `queries`: every entry lies in this range. `latent_cache`: every entry lies in this range. `route_ids`: each row names 8 different experts; every expert is named by at most 384 rows, and one expert by exactly 384. `cache_len`: some row has exactly 128 filled positions.
All inputs are finite; a program needn't handle non-finite values. No bound on the sum of `cache_len` on one device may be relied on, other than what follows from the above.
Results may differ from the reference program's by a relative error of at most 0.018.
Values may be sent and summed in bfloat16 or wider, within the bound.
No kernel may reach another device: no remote copies, remote signals or barrier semaphores. Data moves between devices by JAX's collectives and lax.ppermute only.
A program may use at most 128 MiB of HBM per device.

```python
import math
import jax
import jax.numpy as jnp
import numpy as np
from jax import lax

D = 7168
HEADS = 128
LAT = 512
ROPE = 64
VDIM = 128
FF = 2048
TOP = 8
CACHE = 128
ROWS = 512
EXPERTS = 16
CAP = 384


def attention_inputs(key):
    cache_key = jax.random.fold_in(key, 11)
    query_key = jax.random.fold_in(key, 23)
    latents = jax.random.truncated_normal(cache_key, -6.0, 6.0, (ROWS, CACHE, LAT + ROPE), jnp.float32)
    query_vals = jax.random.truncated_normal(query_key, -6.0, 6.0, (ROWS, HEADS, LAT + ROPE), jnp.float32)
    return (query_vals, latents)


def draw_queries(key, part):
    query_vals, latents = attention_inputs(key)
    return query_vals.astype(jnp.bfloat16)


def draw_latent_cache(key, part):
    query_vals, latents = attention_inputs(key)
    return latents.astype(jnp.bfloat16)


def strengthened(values, stream_key, source, target, blocks, factor):
    owner, partner = [(jnp.arange(values.shape[axis_at]) // (values.shape[axis_at] // blocks)).reshape([-1 if axis == axis_at else 1 for axis in range(values.ndim)]) for axis_at in (source, target)]
    chosen = jax.random.permutation(stream_key, blocks)[partner]
    strong = (owner == chosen) | (owner == (partner + blocks // 2) % blocks)
    return jnp.where(strong, factor * values, values)


def steps_of(stream_key, dims, pieces, low, top_value):
    def one(position, blocks):
        draws = jax.random.uniform(jax.random.fold_in(jax.random.fold_in(stream_key, 6), position), (blocks,), jnp.float32, low / len(pieces), top_value / len(pieces))
        return jnp.repeat(jnp.exp(draws), dims[position] // blocks).reshape((-1,) + (1,) * (len(dims) - position - 1))

    gain = one(*pieces[0])
    for cut in pieces[1:]:
        gain = gain * one(*cut)
    return gain


def length_profile(amount, total, limit, skew):
    weights = [(1 << 20) // math.isqrt(rank ** skew) + 1 for rank in range(2, amount + 1)]
    rest, counts = total - limit - (amount - 1), [1] * (amount - 1)
    while rest > 0:
        movable = [i for i in range(amount - 1) if counts[i] < limit]
        pool, left = sum([weights[i] for i in movable]), rest
        for i in movable:
            extra = min(limit - counts[i], max(1, left * weights[i] // pool), rest)
            counts[i] = counts[i] + extra
            rest = rest - extra
    return np.array([limit] + counts)


def uneven(stream_key, count, total, bound, slope):
    if count == 2:
        one = jax.random.randint(stream_key, (), max(1, total - bound), min(bound, total - 1) + 1)
        return jnp.stack([one, total - one])
    sizes = jnp.asarray(length_profile(count, total, bound, slope), jnp.int32)
    pairs = (count - 1) // 2
    giver, receiver = sizes[1:1 + 2 * pairs:2], sizes[2:2 + 2 * pairs:2]
    room = jnp.minimum(giver - 1, bound - receiver)
    moved = jax.random.randint(jax.random.fold_in(stream_key, 1), (pairs,), 0, 1 << 20) % (room + 1)
    sizes = sizes.at[1:1 + 2 * pairs:2].set(giver - moved).at[2:2 + 2 * pairs:2].set(receiver + moved)
    return sizes[jax.random.permutation(jax.random.fold_in(stream_key, 2), count)]


def assign_block(stream_key, own, number, rows, amount, top, reach, skew):
    ranking = jax.random.permutation(stream_key, amount)
    packed, ordinary = portions_of(amount, rows * top, reach, skew, True), portions_of(amount, rows * top, reach, skew, False)
    places = jnp.arange(amount)

    def named(sizes, turn):
        used = int((sizes > 0).sum())
        fixed = max(1, used // 4)
        passed = fixed + (places - fixed + turn * (used - fixed)) % max(1, amount - fixed)
        return jnp.zeros((amount,), jnp.int32).at[ranking[jnp.where(places < fixed, places, passed)]].set(jnp.asarray(sizes, jnp.int32))

    sizes = jnp.where(number % 4 == 0, named(packed, number // 4), named(ordinary, number - number // 4 - 1))
    mixed = jax.random.permutation(jax.random.fold_in(own, 3), amount)
    giver, sink = mixed[0:amount // 2 * 2:2], mixed[1:amount // 2 * 2:2]
    slack = jnp.minimum(sizes[giver] - 1, reach - sizes[sink]) // 2
    slack = jnp.where((giver == ranking[0]) | (sink == ranking[0]) | (sizes[sink] == 0), 0, jnp.maximum(slack, 0))
    passed = jax.random.randint(jax.random.fold_in(own, 4), (amount // 2,), 0, 1 << 20) % (slack + 1)
    sizes = sizes.at[giver].add(-passed).at[sink].add(passed)
    items = jnp.searchsorted(jnp.cumsum(sizes), jnp.arange(rows * top), side="right").astype(jnp.int32)
    table = items.reshape(top, rows).T
    table = table[jax.random.permutation(jax.random.fold_in(own, 1), rows)]
    turn = jax.random.randint(jax.random.fold_in(own, 2), (rows, 1), 0, top)
    return jnp.take_along_axis(table, (jnp.arange(top)[None, :] + turn) % top, axis=1)


def portions_of(amount, total, reach, slope, full):
    weights = [(1 << 20) // math.isqrt(rank ** slope) + 1 for rank in range(1, amount + 1)]
    largest = reach if full else min(reach, max(-(-total // amount), total * weights[0] // sum(weights)))
    least = 1 if total - largest >= amount - 1 else 0
    holding, surplus = [largest] + [least] * (amount - 1), total - largest - least * (amount - 1)
    while surplus > 0:
        free = [i for i in range(1, amount) if holding[i] < largest] or [i for i in range(1, amount) if holding[i] < reach]
        whole, left = sum([weights[i] for i in free]), surplus
        for i in free:
            more = min(reach - holding[i], max(1, left * weights[i] // whole), surplus)
            holding[i] = holding[i] + more
            surplus = surplus - more
    return np.array(holding)


def normal_values(own_key, dims, spread, reach, pieces=(), held_as=jnp.bfloat16):
    factor_of = steps_of(own_key, dims, pieces, -0.22, 0.18) if pieces else 1.0
    drawn = jax.random.normal(own_key, dims, jnp.float32) * spread * factor_of
    return jnp.minimum(jnp.maximum(drawn, -reach), reach).astype(held_as)


def heavy_noise(rng, extent, spread, limit, cuts, heavy, kind=jnp.bfloat16):
    values = spread * jax.random.normal(rng, extent, jnp.float32)
    if cuts:
        values = values * steps_of(rng, extent, cuts, -0.22, 0.18)
    return jnp.clip(strengthened(values, jax.random.fold_in(rng, 3), *heavy), -limit, limit).astype(kind)


def setup_inputs(seed: int = 0) -> dict:
    keys = jax.random.split(jax.random.key(seed), 12)
    queries = draw_queries(jax.random.fold_in(keys[11], 71), 0)
    latent_cache = draw_latent_cache(jax.random.fold_in(keys[11], 71), 0)
    cache_len = uneven(keys[2], ROWS, ROWS * CACHE // 2, CACHE, 2).astype(jnp.int32)
    value_up = normal_values(keys[3], (HEADS, LAT, VDIM), LAT ** -0.5, 0.25, ((0, 2),))
    out_proj = normal_values(keys[4], (HEADS * VDIM, D), (HEADS * VDIM) ** -0.5, 0.046875, ((0, 2), (1, 16)))
    residual = normal_values(keys[5], (ROWS, D), 0.5, 3.0, ((1, 16),))
    w_gate = normal_values(keys[6], (EXPERTS, D, FF), D ** -0.5, 0.0625, ((0, 16), (2, 2)))
    w_up = normal_values(keys[7], (EXPERTS, D, FF), D ** -0.5, 0.0625, ((0, 16), (2, 2)))
    w_down = heavy_noise(keys[8], (EXPERTS, FF, D), FF ** -0.5, 0.1875, ((0, 16), (1, 2)), (0, 2, 16, 2.0))
    route_ids_keys = jax.random.split(jax.random.fold_in(keys[9], 1), ROWS // ROWS)
    route_ids_turns = jax.random.permutation(jax.random.fold_in(keys[9], 3), ROWS // ROWS)
    route_ids = jax.vmap(lambda own, number: assign_block(jax.random.fold_in(keys[9], 2), own, number, ROWS, EXPERTS, TOP, CAP, 2))(route_ids_keys, route_ids_turns).reshape((ROWS, TOP))
    route_weights = jnp.clip(jnp.exp(jax.random.uniform(keys[10], (ROWS, TOP), jnp.float32, math.log(0.1), math.log(0.6))), 0.1, 0.6)
    return dict(queries=queries, latent_cache=latent_cache, cache_len=cache_len, value_up=value_up, out_proj=out_proj, residual=residual, w_gate=w_gate, w_up=w_up, w_down=w_down, route_ids=route_ids, route_weights=route_weights)


SOFTMAX_SCALE = 0.0721688
MASK_VALUE = -1e30


def reference(queries, latent_cache, cache_len, value_up, out_proj, residual, w_gate, w_up, w_down, route_ids, route_weights):
    query_f = queries.astype(jnp.float32)
    cache_f = latent_cache.astype(jnp.float32)
    scores = jnp.einsum("rhk,rlk->rhl", query_f, cache_f) * SOFTMAX_SCALE
    positions = jnp.arange(CACHE, dtype=jnp.int32)
    in_range = positions[None, None, :] < cache_len[:, None, None]
    masked = jnp.where(in_range, scores, MASK_VALUE)
    row_max = jnp.max(masked, axis=2, keepdims=True)
    exp_scores = jnp.where(in_range, jnp.exp(masked - row_max), 0.0)
    probs = (exp_scores / jnp.sum(exp_scores, axis=2, keepdims=True)).astype(jnp.bfloat16)
    latent_out = jnp.einsum("rhl,rlc->rhc", probs.astype(jnp.float32), cache_f[:, :, :LAT]).astype(jnp.bfloat16)
    heads_out = jnp.einsum("rhc,hcv->rhv", latent_out.astype(jnp.float32), value_up.astype(jnp.float32))
    heads_out = heads_out.astype(jnp.bfloat16).reshape(ROWS, HEADS * VDIM)
    attention = jnp.dot(heads_out, out_proj, preferred_element_type=jnp.float32)
    layer_input = (residual.astype(jnp.float32) + attention).astype(jnp.bfloat16)

    def expert_step(running, expert_index):
        matches = route_ids == expert_index
        weight = jnp.sum(jnp.where(matches, route_weights, 0.0), axis=1)
        gate_value = jnp.dot(layer_input, w_gate[expert_index], preferred_element_type=jnp.float32)
        up_value = jnp.dot(layer_input, w_up[expert_index], preferred_element_type=jnp.float32)
        hidden = (weight[:, None] * jax.nn.silu(gate_value) * up_value).astype(jnp.bfloat16)
        return running + jnp.dot(hidden, w_down[expert_index], preferred_element_type=jnp.float32), None

    routed, _ = lax.scan(expert_step, jnp.zeros((ROWS, D), jnp.float32), jnp.arange(EXPERTS, dtype=jnp.int32))
    return (layer_input.astype(jnp.float32) + routed).astype(jnp.bfloat16)
```

```python
import functools

import jax
import jax.numpy as jnp
from jax import lax
from jax.experimental import pallas as pl
from jax.experimental.pallas import tpu as pltpu
from jax.sharding import Mesh
from jax.sharding import PartitionSpec as P

LAT = 512
VDIM = 128
SOFTMAX_SCALE = 0.0721688
MASK_VALUE = -1e30
MIB = 1024 * 1024

GRP = ("line", "side", "core")
HID = ("sect", "tp")
F32 = jnp.float32
BF16 = jnp.bfloat16


def swap(value, axis):
    return lax.ppermute(value, axis, [(0, 1), (1, 0)])


def shift(value, amount):
    size = lax.axis_size("line")
    return lax.ppermute(value, "line", [(i, (i + amount) % size) for i in range(size)])


def relative(value, axis, index):
    return jnp.where(index == 0, value, jnp.flip(value, axis))


def attend(queries, latent_cache, cache_len, value_up):
    scores = (
        jnp.einsum("rhk,rlk->rhl", queries, latent_cache, preferred_element_type=F32)
        * SOFTMAX_SCALE
    )
    positions = jnp.arange(latent_cache.shape[1], dtype=jnp.int32)
    in_range = positions[None, None, :] < cache_len[:, None, None]
    masked = jnp.where(in_range, scores, MASK_VALUE)
    row_max = jnp.max(masked, axis=2, keepdims=True)
    exp_scores = jnp.where(in_range, jnp.exp(masked - row_max), 0.0)
    probs = (exp_scores / jnp.sum(exp_scores, axis=2, keepdims=True)).astype(BF16)
    latent_out = jnp.einsum(
        "rhl,rlc->rhc", probs, latent_cache[:, :, :LAT], preferred_element_type=F32
    ).astype(BF16)
    heads_out = jnp.einsum("rhc,hcv->rhv", latent_out, value_up, preferred_element_type=F32)
    return heads_out.astype(BF16).reshape(queries.shape[0], queries.shape[1] * VDIM)


def in_hbm(value):
    return pltpu.with_memory_space_constraint(value, pltpu.HBM)


def project_kernel(count, place_ref, own_ref, sibling_ref, *refs):
    blocks, refs = refs[:-8], refs[-8:]
    out_ref, rows_ref, own_rows, sibling_rows, own_total, sibling_total, total_ref, arrived = refs
    size, depth = blocks[0].shape
    tile = min(1024, depth)
    tiles = depth // tile

    def rows_copy(i, block):
        start = pl.multiple_of(place_ref[2 * i + 1] * size, size)
        return pltpu.make_async_copy(block, rows_ref.at[pl.ds(start, size)], arrived.at[i])

    def weight_copy(half, k):
        columns = pl.ds(pl.multiple_of(k * tile, tile), tile)
        source, target = ((own_ref, own_rows), (sibling_ref, sibling_rows))[half]
        return pltpu.make_async_copy(
            source.at[:, columns], target.at[:, columns], arrived.at[count + half * tiles + k]
        )

    for i in range(count):
        for at, block in enumerate(blocks):

            @pl.when(place_ref[2 * i] == at)
            def _():
                rows_copy(i, block).start()

    for k in range(tiles):
        for half in range(2):
            weight_copy(half, k).start()
    own_total[...] = jnp.zeros_like(own_total)
    sibling_total[...] = jnp.zeros_like(sibling_total)
    for i in range(count):
        rows_copy(i, blocks[0]).wait()

    def step(k, _):
        columns = pl.ds(pl.multiple_of(k * tile, tile), tile)
        rows = rows_ref[:, columns]
        for half, (weight_ref, sum_ref) in enumerate(
            ((own_rows, own_total), (sibling_rows, sibling_total))
        ):
            weight_copy(half, k).wait()
            sum_ref[...] += lax.dot_general(
                weight_ref[:, columns], rows, (((1,), (1,)), ((), ())), preferred_element_type=F32
            )
        return 0

    lax.fori_loop(0, tiles, step, 0)
    width, core = own_total.shape[0], place_ref[2 * count]
    total_ref[pl.ds(pl.multiple_of(core * width, 8), width), :] = own_total[...]
    total_ref[pl.ds(pl.multiple_of((1 - core) * width, 8), width), :] = sibling_total[...]
    out_ref[...] = total_ref[...].T.astype(out_ref.dtype)


def project(place, count, blocks, own, sibling, dtype):
    size, depth = blocks[0].shape
    width = own.shape[0]
    anywhere = pl.BlockSpec(memory_space=pl.ANY)
    return pl.pallas_call(
        functools.partial(project_kernel, count),
        in_specs=[pl.BlockSpec(memory_space=pltpu.SMEM)] + [anywhere] * (2 + len(blocks)),
        out_specs=pl.BlockSpec(memory_space=pltpu.VMEM),
        out_shape=jax.ShapeDtypeStruct((count * size, 2 * width), dtype),
        scratch_shapes=[pltpu.VMEM((count * size, depth), BF16)]
        + [pltpu.VMEM((width, depth), BF16)] * 2
        + [pltpu.VMEM((width, count * size), F32)] * 2
        + [
            pltpu.VMEM((2 * width, count * size), F32),
            pltpu.SemaphoreType.DMA((count + 2 * (depth // min(1024, depth)),)),
        ],
        compiler_params=pltpu.CompilerParams(vmem_limit_bytes=28 * MIB),
        cost_estimate=pl.CostEstimate(
            flops=4 * count * size * depth * width,
            bytes_accessed=2 * depth * (2 * width + count * size),
            transcendentals=0,
        ),
    )(place, in_hbm(own), in_hbm(sibling), *blocks)


def hidden_kernel(layout, first, last, place_ref, *refs):
    total, count = 1 + max(copy[0] for unit in layout for copy in unit), len(layout)
    pieces, (gate_ref, up_ref, *rest) = refs[:total], refs[total:]
    if not first:
        gate_in, up_in, *rest = rest
    if last:
        weight_ref, hidden_ref, *rest = rest
    else:
        gate_out, up_out, *rest = rest
    rows_ref, gate_rows, up_rows, *rest, arrived, fetched, summed = rest
    sums = rest
    size, width = pieces[0].shape[1:]
    depth, columns = 2 * width, gate_ref.shape[1]
    tile = min(512, columns)
    copies = []
    for start, unit in enumerate(layout):
        for piece, entry, row, side in unit:
            column = pl.multiple_of(start * depth + (place_ref[count] + side) % 2 * width, 128)
            copies.append(
                pltpu.make_async_copy(
                    pieces[piece].at[entry],
                    rows_ref.at[pl.ds(row * size, size), pl.ds(column, width)],
                    arrived.at[len(copies)],
                )
            )

    def weight_copies(n, matrix):
        part = pl.ds(pl.multiple_of(n * tile, tile), tile)
        source, target = ((gate_ref, gate_rows), (up_ref, up_rows))[matrix]
        return [
            pltpu.make_async_copy(
                source.at[pl.ds(pl.multiple_of(place_ref[i] * depth + j * width, width), width), part],
                target.at[pl.ds(i * depth + j * width, width), part],
                fetched.at[n, matrix, i, j],
            )
            for i in range(count)
            for j in range(2)
        ]

    def sum_copy(n, matrix, out):
        part = pl.ds(pl.multiple_of(n * tile, tile), tile)
        here = sums[matrix].at[:, part]
        if out:
            there = (gate_out, up_out)[matrix].at[:, part]
            return pltpu.make_async_copy(here, there, summed.at[n, matrix, 1])
        there = (gate_in, up_in)[matrix].at[:, part]
        return pltpu.make_async_copy(there, here, summed.at[n, matrix, 0])

    steps = columns // tile
    for copy in copies:
        copy.start()
    for n in range(steps):
        for matrix in range(2):
            for copy in weight_copies(n, matrix):
                copy.start()
            if not first:
                sum_copy(n, matrix, False).start()
    for copy in copies:
        copy.wait()

    def step(n, _):
        inner = min(256, tile)
        for matrix in range(2):
            for copy in weight_copies(n, matrix):
                copy.wait()
            if not first:
                sum_copy(n, matrix, False).wait()
            for start in range(0, tile, inner):
                part = pl.ds(pl.multiple_of(n * tile + start, inner), inner)
                value = jnp.dot(
                    rows_ref[...], (gate_rows, up_rows)[matrix][:, part], preferred_element_type=F32
                )
                if not first:
                    value += sums[matrix][:, part]
                if last and matrix:
                    gate = sums[0][:, part]
                    hidden_ref[:, part] = (
                        weight_ref[...] * (gate / (1.0 + jnp.exp(-gate))) * value
                    ).astype(hidden_ref.dtype)
                else:
                    sums[matrix][:, part] = value
            if not last:
                sum_copy(n, matrix, True).start()
        return 0

    lax.fori_loop(0, steps, step, 0)
    if not last:
        for n in range(steps):
            for matrix in range(2):
                sum_copy(n, matrix, True).wait()


def hidden_part(units, places, side, pieces, w_gate, w_up, sums=None, weight=None):
    first, last = sums is None, weight is not None
    size, width = pieces[0].shape[1:]
    rows, columns, depth = 4 * size, w_gate.shape[1], 2 * width
    layout, piece = [], 0
    for unit in units:
        layout.append([])
        for core in range(2):
            for place_of in unit:
                for at, (sect, near) in enumerate(place_of):
                    layout[-1].append((piece, at, core * 2 + sect, near))
                piece += 1
    anywhere, vmem = pl.BlockSpec(memory_space=pl.ANY), pl.BlockSpec(memory_space=pltpu.VMEM)
    in_specs = [pl.BlockSpec(memory_space=pltpu.SMEM)] + [anywhere] * (len(pieces) + 2)
    operands = list(pieces) + [in_hbm(w_gate), in_hbm(w_up)]
    if not first:
        in_specs += [anywhere] * 2
        operands += list(sums)
    if last:
        in_specs += [vmem]
        operands += [weight]
        out_shape, out_specs = jax.ShapeDtypeStruct((rows, columns), BF16), vmem
    else:
        out_shape = [jax.ShapeDtypeStruct((rows, columns), F32)] * 2
        out_specs = [anywhere] * 2
    steps = columns // min(512, columns)
    return pl.pallas_call(
        functools.partial(hidden_kernel, layout, first, last),
        in_specs=in_specs,
        out_specs=out_specs,
        out_shape=out_shape,
        scratch_shapes=[pltpu.VMEM((rows, len(units) * depth), BF16)]
        + [pltpu.VMEM((len(units) * depth, columns), BF16)] * 2
        + [pltpu.VMEM((rows, columns), F32)] * 2
        + [
            pltpu.SemaphoreType.DMA((sum(len(unit) for unit in layout),)),
            pltpu.SemaphoreType.DMA((steps, 2, len(units), 2)),
            pltpu.SemaphoreType.DMA((steps, 2, 2)),
        ],
        compiler_params=pltpu.CompilerParams(vmem_limit_bytes=(12 + 10 * len(units)) * MIB),
        cost_estimate=pl.CostEstimate(
            flops=4 * rows * len(units) * depth * columns,
            bytes_accessed=4 * len(units) * depth * columns,
            transcendentals=rows * columns,
        ),
    )(jnp.stack(places + [side]).astype(jnp.int32), *operands)


def add(one, other):
    return (one.astype(F32) + other.astype(F32)).astype(BF16)


def on_device(
    queries,
    latent_cache,
    cache_len,
    value_up,
    out_proj,
    residual,
    w_gate,
    w_up,
    w_down,
    route_ids,
    route_weights,
):
    line = lax.axis_size("line")
    tp = lax.axis_size("tp")
    sect, at, side, core = (lax.axis_index(name) for name in ("sect", "line", "side", "core"))
    block = queries.shape[0]
    row_total, width = residual.shape
    chip_width = 2 * width
    shifts = list(range(line))

    own_proj = out_proj.T
    sibling_proj = swap(own_proj, "core")
    residual_rows = lax.dynamic_slice_in_dim(
        residual.reshape(line, 2, 2, block, width), sect * (line // 2), line // 2, 0
    )
    mine = lax.dynamic_index_in_dim(residual_rows, core, 2, keepdims=False)
    other = swap(lax.dynamic_index_in_dim(residual_rows, 1 - core, 2, keepdims=False), "core")
    residual_rows = jnp.where(
        core == 0, jnp.concatenate([mine, other], axis=3), jnp.concatenate([other, mine], axis=3)
    ).reshape(-1, chip_width)

    heads = attend(queries, latent_cache, cache_len, value_up)
    rights, lefts = [heads], [heads]
    for k in shifts[1:]:
        rights.append(
            lax.ppermute(rights[-1], "line", [(i, i + 1) for i in range(k - 1, line - 1)])
        )
        lefts.append(lax.ppermute(lefts[-1], "line", [(i, i - 1) for i in range(1, line - k + 1)]))
    near = [heads] + [value for pair in zip(rights[1:], lefts[1:]) for value in pair]
    holders = [range(line)] + [
        value for k in shifts[1:] for value in (range(k, line), range(line - k))
    ]
    far = [
        lax.ppermute(value, ("line", "side"), [(2 * i + y, 2 * i + 1 - y) for i in held for y in range(2)])
        for value, held in zip(near, holders)
    ]
    place = []
    for k in shifts:
        origin = jnp.where(at >= k, 2 * k - 1, 2 * (line - k)) if k else 0
        for y in range(2):
            place += [origin + y * len(near), 2 * ((at - k) % line) + (side + y) % 2]
    place = jnp.stack([jnp.int32(value) for value in place] + [core]).astype(jnp.int32)
    partial = project(
        place, 2 * line, near + far, own_proj, sibling_proj, F32 if tp > 1 else BF16
    )
    if tp > 1:
        partial = lax.psum(partial, "tp").astype(BF16)
    partial = partial.reshape(2, -1, chip_width)
    kept = lax.dynamic_index_in_dim(partial, sect, 0, keepdims=False)
    given = lax.dynamic_index_in_dim(partial, 1 - sect, 0, keepdims=False)
    attention = kept.astype(F32) + swap(given, "sect").astype(F32)
    own_rows = (residual_rows.astype(F32) + attention).astype(BF16)

    weight = jnp.sum(jnp.where(route_ids == lax.axis_index(GRP), route_weights, 0.0), axis=1)
    weight = weight.reshape(2, line // 2, 2, 2, block).transpose(3, 0, 1, 2, 4)
    weight = relative(relative(weight, 0, core), 1, sect).reshape(row_total, 1)
    got = {k: shift(own_rows, k) if k else own_rows for k in shifts if k != line // 2}
    right = lax.ppermute(got[1], "line", [(i, i + 1) for i in range(1, line - 1)])
    left = lax.ppermute(got[line - 1], "line", [(i, i - 1) for i in range(1, line - 1)])
    got[line // 2] = jnp.where(at >= line // 2, right, left)
    pairs, opposites = {}, {}
    half, back = line // 2, line - 1
    for k in (0, back, 1, half):
        first, second = ("sect", "side") if k % 2 == 0 else ("side", "sect")
        pairs[k] = jnp.stack([got[k], swap(got[k], first)])
        opposites[k] = swap(pairs[k], second)
    layout = [
        [[(0, 0), (1, 0)], [(0, 1), (1, 1)]] if k % 2 == 0 else [[(0, 0), (0, 1)], [(1, 0), (1, 1)]]
        for k in shifts
    ]
    sums = None
    for group in ([0], [back], [1, half]):
        if group == [back]:
            late = [opposites[k] for k in (back, 1, half)]
            late, sums = lax.optimization_barrier((late, sums))
            opposites.update(zip((back, 1, half), late))
        sums = hidden_part(
            [layout[k] for k in group],
            [(at - k) % line for k in group],
            side,
            [
                piece
                for k in group
                for piece in (
                    pairs[k], opposites[k], swap(pairs[k], "core"), swap(opposites[k], "core")
                )
            ],
            w_gate[0],
            w_up[0],
            sums,
            weight if half in group else None,
        )
    hidden = sums

    def own_side(value):
        return lax.dynamic_slice_in_dim(value, side * chip_width, chip_width, value.ndim - 1)

    def other_side(value):
        return lax.dynamic_slice_in_dim(value, (1 - side) * chip_width, chip_width, value.ndim - 1)

    count = row_total // 2
    send, keep = (
        jnp.dot(rows, w_down[0], preferred_element_type=F32) for rows in (hidden[count:], hidden[:count])
    )
    if tp > 1:
        send, keep = (lax.psum(v, "tp") for v in (send, keep))
    send, keep = send.astype(BF16), keep.astype(BF16)

    def columns_to(value, k):
        return lax.dynamic_slice_in_dim(value, (at + k) % line * 2 * chip_width, 2 * chip_width, 1)

    total, held = own_rows.astype(F32), None
    for group in ((half, 1), (back, 0)):
        arrived = swap(jnp.stack([columns_to(send, k) for k in group]), "core")
        if held is not None:
            arrived, held = lax.optimization_barrier((arrived, held))
        for k, arrival in zip(group, arrived):
            part = add(columns_to(keep, k), arrival).reshape(2, -1, 2 * chip_width)
            if k % 2 == 0:
                part = add(part[0], swap(part[1], "sect"))
                held = part
                part = add(own_side(part), swap(other_side(part), "side"))
            else:
                part = add(own_side(part), swap(other_side(part), "side"))
                part = add(part[0], swap(part[1], "sect"))
            total = total + (shift(part, k) if k else part).astype(F32)
    total = total.astype(BF16)

    mine = jnp.where(core == 0, total[:, :width], total[:, width:])
    other = swap(jnp.where(core == 0, total[:, width:], total[:, :width]), "core")
    out = relative(jnp.stack([mine, other]), 0, core).reshape(2, -1, block, width)
    out = out.transpose(1, 0, 2, 3).reshape(-1, width)
    share = out.shape[0] // tp
    return lax.dynamic_slice_in_dim(out, lax.axis_index("tp") * share, share, 0)


def solution(mesh):
    sizes = dict(mesh.shape)
    fine = Mesh(
        mesh.devices.reshape(sizes["sect"], sizes["grp"] // 4, 2, 2, sizes["tp"]),
        ("sect", "line", "side", "core", "tp"),
    )
    return jax.shard_map(
        on_device,
        mesh=fine,
        in_specs=(
            P(GRP, HID, None),
            P(GRP, None, None),
            P(GRP),
            P(HID, None, None),
            P(HID, GRP),
            P(None, GRP),
            P(GRP, None, HID),
            P(GRP, None, HID),
            P(GRP, HID, None),
            P(),
            P(),
        ),
        out_specs=P(HID, GRP),
        check_vma=False,
    )
```

```python
import functools

import jax
import jax.numpy as jnp
from jax import lax
from jax.experimental import pallas as pl
from jax.experimental.pallas import tpu as pltpu
from jax.sharding import Mesh
from jax.sharding import PartitionSpec as P

LAT = 512
VDIM = 128
SOFTMAX_SCALE = 0.0721688
MASK_VALUE = -1e30
MIB = 1024 * 1024

GRP = ("line", "side", "core")
HID = ("sect", "tp")
F32 = jnp.float32
BF16 = jnp.bfloat16


def swap(value, axis):
    return lax.ppermute(value, axis, [(0, 1), (1, 0)])


def shift(value, amount):
    size = lax.axis_size("line")
    return lax.ppermute(value, "line", [(i, (i + amount) % size) for i in range(size)])


def relative(value, axis, index):
    return jnp.where(index == 0, value, jnp.flip(value, axis))


def in_hbm(value):
    return pltpu.with_memory_space_constraint(value, pltpu.HBM)


def attend_kernel(length_ref, query_ref, cache_ref, out_ref):
    rows, depth = out_ref.shape[0], out_ref.shape[2]
    scores = [
        jnp.dot(query_ref[i], cache_ref[i], preferred_element_type=F32) for i in range(rows)
    ]
    positions = lax.broadcasted_iota(jnp.int32, scores[0].shape, 1)
    probs = []
    for i in range(rows):
        in_range = positions < length_ref[pl.program_id(0) * rows + i]
        masked = jnp.where(in_range, scores[i] * SOFTMAX_SCALE, MASK_VALUE)
        row_max = jnp.max(masked, axis=1, keepdims=True)
        exp_scores = jnp.where(in_range, jnp.exp(masked - row_max), 0.0)
        probs.append((exp_scores / jnp.sum(exp_scores, axis=1, keepdims=True)).astype(BF16))
    latent = [
        lax.dot_general(
            probs[i], cache_ref[i, :depth, :], (((1,), (1,)), ((), ())), preferred_element_type=F32
        )
        for i in range(rows)
    ]
    for i in range(rows):
        out_ref[i] = latent[i].astype(BF16)


def attend(queries, latent_cache, cache_len, value_up):
    rows, heads, depth = queries.shape
    positions = latent_cache.shape[1]
    tile = 8
    latent_out = pl.pallas_call(
        attend_kernel,
        grid_spec=pltpu.PrefetchScalarGridSpec(
            num_scalar_prefetch=1,
            grid=(rows // tile,),
            in_specs=[
                pl.BlockSpec((tile, heads, depth), lambda r, length: (r, 0, 0)),
                pl.BlockSpec((tile, depth, positions), lambda r, length: (r, 0, 0)),
            ],
            out_specs=pl.BlockSpec((tile, heads, LAT), lambda r, length: (r, 0, 0)),
        ),
        out_shape=jax.ShapeDtypeStruct((rows, heads, LAT), BF16),
        compiler_params=pltpu.CompilerParams(vmem_limit_bytes=16 * MIB),
        cost_estimate=pl.CostEstimate(
            flops=2 * rows * heads * positions * (depth + LAT),
            bytes_accessed=2 * rows * (heads * (depth + LAT) + positions * depth),
            transcendentals=rows * heads * positions,
        ),
    )(cache_len, in_hbm(queries), in_hbm(latent_cache.transpose(0, 2, 1)))
    heads_out = jnp.einsum("rhc,hcv->rhv", latent_out, value_up, preferred_element_type=F32)
    return heads_out.astype(BF16).reshape(rows, heads * VDIM)


def project_kernel(slots, start, first, place_ref, own_ref, sibling_ref, *refs):
    blocks, (out_ref, rows_ref, weight_ref, total_ref, arrived) = refs[:-5], refs[-5:]
    if not first:
        earlier_ref, *blocks = blocks
    count, (size, depth), width = len(slots), blocks[0].shape, own_ref.shape[0]
    tile = min(2048, depth)
    tiles = depth // tile

    def rows_copy(i, block):
        start = pl.multiple_of(place_ref[2 * i + 1] * size, size)
        return pltpu.make_async_copy(block, rows_ref.at[pl.ds(start, size)], arrived.at[i])

    def weight_copy(half, k):
        columns = pl.ds(pl.multiple_of(k * tile, tile), tile)
        source, place = ((own_ref, place_ref[2 * count]), (sibling_ref, 1 - place_ref[2 * count]))[half]
        return pltpu.make_async_copy(
            source.at[:, pl.ds(pl.multiple_of(start + k * tile, tile), tile)],
            weight_ref.at[pl.ds(pl.multiple_of(place * width, 16), width), columns],
            arrived.at[count + half * tiles + k],
        )

    for i, slot in enumerate(slots):
        if len(slot) == 1:
            rows_copy(i, blocks[slot[0]]).start()
            continue
        from_left = place_ref[2 * i] == 1

        @pl.when(from_left)
        def _():
            rows_copy(i, blocks[slot[0]]).start()

        @pl.when(jnp.logical_not(from_left))
        def _():
            rows_copy(i, blocks[slot[1]]).start()

    for k in range(tiles):
        for half in range(2):
            weight_copy(half, k).start()
    total_ref[...] = jnp.zeros_like(total_ref)
    for i in range(count):
        rows_copy(i, blocks[0]).wait()

    def step(k, _):
        columns = pl.ds(pl.multiple_of(k * tile, tile), tile)
        for half in range(2):
            weight_copy(half, k).wait()
        total_ref[...] += lax.dot_general(
            weight_ref[:, columns],
            rows_ref[:, columns],
            (((1,), (1,)), ((), ())),
            preferred_element_type=F32,
        )
        return 0

    lax.fori_loop(0, tiles, step, 0)
    total = total_ref[...].T
    if not first:
        total = total + earlier_ref[...]
    out_ref[...] = total.astype(out_ref.dtype)


def project(place, slots, blocks, own, sibling, start, earlier, dtype):
    vmem = pl.BlockSpec(memory_space=pltpu.VMEM)
    first = earlier is None
    count, (size, depth) = len(slots), blocks[0].shape
    width = own.shape[0]
    anywhere = pl.BlockSpec(memory_space=pl.ANY)
    return pl.pallas_call(
        functools.partial(project_kernel, slots, start, first),
        in_specs=[pl.BlockSpec(memory_space=pltpu.SMEM)]
        + [anywhere] * 2
        + ([] if first else [vmem])
        + [anywhere] * len(blocks),
        out_specs=vmem,
        out_shape=jax.ShapeDtypeStruct((count * size, 2 * width), dtype),
        scratch_shapes=[
            pltpu.VMEM((count * size, depth), BF16),
            pltpu.VMEM((2 * width, depth), BF16),
            pltpu.VMEM((2 * width, count * size), F32),
            pltpu.SemaphoreType.DMA((count + 2 * (depth // min(2048, depth)),)),
        ],
        compiler_params=pltpu.CompilerParams(vmem_limit_bytes=16 * MIB),
        cost_estimate=pl.CostEstimate(
            flops=4 * count * size * depth * width,
            bytes_accessed=2 * depth * (2 * width + count * size),
            transcendentals=0,
        ),
    )(place, in_hbm(own), in_hbm(sibling), *([] if first else [earlier]), *blocks)


def hidden_kernel(layout, first, last, place_ref, *refs):
    total, count = 1 + max(copy[0] for unit in layout for copy in unit), len(layout)
    pieces, (gate_ref, up_ref, *rest) = refs[:total], refs[total:]
    if not first:
        gate_in, up_in, *rest = rest
    if last:
        weight_ref, hidden_ref, *rest = rest
    else:
        gate_out, up_out, *rest = rest
    rows_ref, gate_rows, up_rows, *rest, arrived, fetched, summed = rest
    sums = rest
    size, width = pieces[0].shape[1:]
    depth, columns = 2 * width, gate_ref.shape[1]
    tile = min(512, columns)
    copies = []
    for start, unit in enumerate(layout):
        for piece, entry, row, side in unit:
            column = pl.multiple_of(start * depth + (place_ref[count] + side) % 2 * width, 128)
            copies.append(
                pltpu.make_async_copy(
                    pieces[piece].at[entry],
                    rows_ref.at[pl.ds(row * size, size), pl.ds(column, width)],
                    arrived.at[len(copies)],
                )
            )

    def weight_copies(n, matrix):
        part = pl.ds(pl.multiple_of(n * tile, tile), tile)
        source, target = ((gate_ref, gate_rows), (up_ref, up_rows))[matrix]
        return [
            pltpu.make_async_copy(
                source.at[pl.ds(pl.multiple_of(place_ref[i] * depth + j * width, width), width), part],
                target.at[pl.ds(i * depth + j * width, width), part],
                fetched.at[n, matrix, i, j],
            )
            for i in range(count)
            for j in range(2)
        ]

    def sum_copy(n, matrix, out):
        part = pl.ds(pl.multiple_of(n * tile, tile), tile)
        here = sums[matrix].at[:, part]
        if out:
            there = (gate_out, up_out)[matrix].at[:, part]
            return pltpu.make_async_copy(here, there, summed.at[n, matrix, 1])
        there = (gate_in, up_in)[matrix].at[:, part]
        return pltpu.make_async_copy(there, here, summed.at[n, matrix, 0])

    steps = columns // tile
    for copy in copies:
        copy.start()
    for n in range(steps):
        for matrix in range(2):
            for copy in weight_copies(n, matrix):
                copy.start()
            if not first:
                sum_copy(n, matrix, False).start()
    for copy in copies:
        copy.wait()

    def step(n, _):
        inner = min(256, tile)
        for matrix in range(2):
            for copy in weight_copies(n, matrix):
                copy.wait()
            if not first:
                sum_copy(n, matrix, False).wait()
            for start in range(0, tile, inner):
                part = pl.ds(pl.multiple_of(n * tile + start, inner), inner)
                value = jnp.dot(
                    rows_ref[...], (gate_rows, up_rows)[matrix][:, part], preferred_element_type=F32
                )
                if not first:
                    value += sums[matrix][:, part]
                if last and matrix:
                    gate = sums[0][:, part]
                    hidden_ref[:, part] = (
                        weight_ref[:, :1] * (gate / (1.0 + jnp.exp(-gate))) * value
                    ).astype(hidden_ref.dtype)
                else:
                    sums[matrix][:, part] = value
            if not last:
                sum_copy(n, matrix, True).start()
        return 0

    lax.fori_loop(0, steps, step, 0)
    if not last:
        for n in range(steps):
            for matrix in range(2):
                sum_copy(n, matrix, True).wait()


def hidden_part(units, places, pieces, w_gate, w_up, sums=None, weight=None):
    first, last = sums is None, weight is not None
    size, width = pieces[0].shape[1:]
    rows, columns, depth = 4 * size, w_gate.shape[1], 2 * width
    layout, piece = [], 0
    for unit in units:
        layout.append([])
        for core in range(2):
            for place_of in unit:
                for at, (sect, near) in enumerate(place_of):
                    layout[-1].append((piece, at, core * 2 + sect, near))
                piece += 1
    anywhere, vmem = pl.BlockSpec(memory_space=pl.ANY), pl.BlockSpec(memory_space=pltpu.VMEM)
    in_specs = [pl.BlockSpec(memory_space=pltpu.SMEM)] + [anywhere] * (len(pieces) + 2)
    operands = list(pieces) + [in_hbm(w_gate), in_hbm(w_up)]
    if not first:
        in_specs += [anywhere] * 2
        operands += list(sums)
    if last:
        in_specs += [vmem]
        operands += [weight]
        out_shape, out_specs = jax.ShapeDtypeStruct((rows, columns), BF16), vmem
    else:
        out_shape = [jax.ShapeDtypeStruct((rows, columns), F32)] * 2
        out_specs = [anywhere] * 2
    steps = columns // min(512, columns)
    return pl.pallas_call(
        functools.partial(hidden_kernel, layout, first, last),
        in_specs=in_specs,
        out_specs=out_specs,
        out_shape=out_shape,
        scratch_shapes=[pltpu.VMEM((rows, len(units) * depth), BF16)]
        + [pltpu.VMEM((len(units) * depth, columns), BF16)] * 2
        + [pltpu.VMEM((rows, columns), F32)] * 2
        + [
            pltpu.SemaphoreType.DMA((sum(len(unit) for unit in layout),)),
            pltpu.SemaphoreType.DMA((steps, 2, len(units), 2)),
            pltpu.SemaphoreType.DMA((steps, 2, 2)),
        ],
        compiler_params=pltpu.CompilerParams(vmem_limit_bytes=(12 + 10 * len(units)) * MIB),
        cost_estimate=pl.CostEstimate(
            flops=4 * rows * len(units) * depth * columns,
            bytes_accessed=4 * len(units) * depth * columns,
            transcendentals=rows * columns,
        ),
    )(places, *operands)


def add(one, other):
    return (one.astype(F32) + other.astype(F32)).astype(BF16)


def on_device(
    queries,
    latent_cache,
    cache_len,
    value_up,
    out_proj,
    residual,
    w_gate,
    w_up,
    w_down,
    route_ids,
    route_weights,
):
    line = lax.axis_size("line")
    tp = lax.axis_size("tp")
    sect, at, side, core = (lax.axis_index(name) for name in ("sect", "line", "side", "core"))
    block = queries.shape[0]
    row_total, width = residual.shape
    chip_width = 2 * width
    shifts = list(range(line))

    own_proj = out_proj.T
    sibling_proj = swap(own_proj, "core")
    residual_rows = lax.dynamic_slice_in_dim(
        residual.reshape(line, 2, 2, block, width), sect * (line // 2), line // 2, 0
    )
    mine = lax.dynamic_index_in_dim(residual_rows, core, 2, keepdims=False)
    other = swap(lax.dynamic_index_in_dim(residual_rows, 1 - core, 2, keepdims=False), "core")
    residual_rows = jnp.where(
        core == 0, jnp.concatenate([mine, other], axis=3), jnp.concatenate([other, mine], axis=3)
    ).reshape(-1, chip_width)

    heads = attend(queries, latent_cache, cache_len, value_up)
    weight = jnp.sum(jnp.where(route_ids == lax.axis_index(GRP), route_weights, 0.0), axis=1)
    weight = weight.reshape(2, line // 2, 2, 2, block).transpose(3, 0, 1, 2, 4)
    weight = relative(relative(weight, 0, core), 1, sect).reshape(row_total, 1)
    weight = jnp.broadcast_to(weight, (row_total, 128))
    holders = [range(line)] + [
        value for k in shifts[1:] for value in (range(k, line), range(line - k))
    ]
    slots, place = [], []
    for k in shifts:
        slot = (2 * k - 1, 2 * (line - k)) if k else (0,)
        for y in range(2):
            slots.append(tuple(i + y * len(holders) for i in slot))
            place += [at >= k, 2 * ((at - k) % line) + (side + y) % 2]
    place = jnp.stack([jnp.asarray(value, jnp.int32) for value in place + [core]])
    half, back = line // 2, line - 1
    groups = ([0], [back], [1, half])
    group_places = [
        jnp.stack([(at - k) % line for k in group] + [side]).astype(jnp.int32) for group in groups
    ]
    length, partial, blocks = heads.shape[1] // 2, None, []
    for part in range(2):
        own = heads[:, part * length : (part + 1) * length]
        if part:
            own, weight, residual_rows, place, group_places = lax.optimization_barrier(
                (own, weight, residual_rows, place, group_places)
            )
        rights, lefts = [own], [own]
        for k in shifts[1:]:
            if k == 3 and not part:
                rights[-1], sibling_proj = lax.optimization_barrier((rights[-1], sibling_proj))
            right = [(i, i + 1) for i in range(k - 1, line - 1)]
            left = [(i, i - 1) for i in range(1, line - k + 1)]
            rights.append(lax.ppermute(rights[-1], "line", right))
            lefts.append(lax.ppermute(lefts[-1], "line", left))
        near = [own] + [value for pair in zip(rights[1:], lefts[1:]) for value in pair]
        far = [
            lax.ppermute(
                value, ("line", "side"), [(2 * i + y, 2 * i + 1 - y) for i in held for y in range(2)]
            )
            for value, held in zip(near, holders)
        ]
        blocks.append(near + far)
    for part in range(2):
        partial = project(
            place,
            slots,
            blocks[part],
            own_proj,
            sibling_proj,
            part * length,
            partial,
            BF16 if part and tp == 1 else F32,
        )
    if tp > 1:
        partial = lax.psum(partial, "tp").astype(BF16)
    partial = partial.reshape(2, -1, chip_width)
    kept = lax.dynamic_index_in_dim(partial, sect, 0, keepdims=False)
    given = lax.dynamic_index_in_dim(partial, 1 - sect, 0, keepdims=False)
    attention = kept.astype(F32) + swap(given, "sect").astype(F32)
    own_rows = (residual_rows.astype(F32) + attention).astype(BF16)

    got = {k: shift(own_rows, k) if k else own_rows for k in shifts if k != line // 2}
    right = lax.ppermute(got[1], "line", [(i, i + 1) for i in range(1, line - 1)])
    left = lax.ppermute(got[line - 1], "line", [(i, i - 1) for i in range(1, line - 1)])
    got[line // 2] = jnp.where(at >= line // 2, right, left)
    pairs, opposites = {}, {}
    for k in (0, back, 1, half):
        first, second = ("sect", "side") if k % 2 == 0 else ("side", "sect")
        pairs[k] = jnp.stack([got[k], swap(got[k], first)])
        opposites[k] = swap(pairs[k], second)
    layout = [
        [[(0, 0), (1, 0)], [(0, 1), (1, 1)]] if k % 2 == 0 else [[(0, 0), (0, 1)], [(1, 0), (1, 1)]]
        for k in shifts
    ]
    sums = None
    for group, places in zip(groups, group_places):
        if group == [back]:
            for k in (back, 1, half):
                opposites[k], _ = lax.optimization_barrier((opposites[k], sums))
        sums = hidden_part(
            [layout[k] for k in group],
            places,
            [
                piece
                for k in group
                for piece in (
                    pairs[k], opposites[k], swap(pairs[k], "core"), swap(opposites[k], "core")
                )
            ],
            w_gate[0],
            w_up[0],
            sums,
            weight if half in group else None,
        )
    hidden = sums

    def own_side(value):
        return lax.dynamic_slice_in_dim(value, side * chip_width, chip_width, value.ndim - 1)

    def other_side(value):
        return lax.dynamic_slice_in_dim(value, (1 - side) * chip_width, chip_width, value.ndim - 1)

    count = row_total // 2
    send, keep = (
        jnp.dot(rows, w_down[0], preferred_element_type=F32) for rows in (hidden[count:], hidden[:count])
    )
    if tp > 1:
        send, keep = (lax.psum(v, "tp") for v in (send, keep))
    send, keep = send.astype(BF16), keep.astype(BF16)

    def columns_to(value, k):
        return lax.dynamic_slice_in_dim(value, (at + k) % line * 2 * chip_width, 2 * chip_width, 1)

    total, held = own_rows.astype(F32), None
    for group in ((half, 1), (back, 0)):
        arrived = swap(jnp.stack([columns_to(send, k) for k in group]), "core")
        if held is not None:
            arrived, held = lax.optimization_barrier((arrived, held))
        for k, arrival in zip(group, arrived):
            part = add(columns_to(keep, k), arrival).reshape(2, -1, 2 * chip_width)
            if k % 2 == 0:
                part = add(part[0], swap(part[1], "sect"))
                held = part
                part = add(own_side(part), swap(other_side(part), "side"))
            else:
                part = add(own_side(part), swap(other_side(part), "side"))
                part = add(part[0], swap(part[1], "sect"))
            total = total + (shift(part, k) if k else part).astype(F32)
    total = total.astype(BF16)

    mine = jnp.where(core == 0, total[:, :width], total[:, width:])
    other = swap(jnp.where(core == 0, total[:, width:], total[:, :width]), "core")
    out = relative(jnp.stack([mine, other]), 0, core).reshape(2, -1, block, width)
    out = out.transpose(1, 0, 2, 3).reshape(-1, width)
    share = out.shape[0] // tp
    return lax.dynamic_slice_in_dim(out, lax.axis_index("tp") * share, share, 0)


def solution(mesh):
    sizes = dict(mesh.shape)
    fine = Mesh(
        mesh.devices.reshape(sizes["sect"], sizes["grp"] // 4, 2, 2, sizes["tp"]),
        ("sect", "line", "side", "core", "tp"),
    )
    return jax.shard_map(
        on_device,
        mesh=fine,
        in_specs=(
            P(GRP, HID, None),
            P(GRP, None, None),
            P(GRP),
            P(HID, None, None),
            P(HID, GRP),
            P(None, GRP),
            P(GRP, None, HID),
            P(GRP, None, HID),
            P(GRP, HID, None),
            P(),
            P(),
        ),
        out_specs=P(HID, GRP),
        check_vma=False,
    )
```

```python
import functools

import jax
import jax.numpy as jnp
from jax import lax
from jax.experimental import pallas as pl
from jax.experimental.pallas import tpu as pltpu
from jax.sharding import Mesh
from jax.sharding import PartitionSpec as P

LAT = 512
VDIM = 128
SOFTMAX_SCALE = 0.0721688
MASK_VALUE = -1e30
MIB = 1024 * 1024

GRP = ("line", "side", "core")
HID = ("sect", "tp")
F32 = jnp.float32
BF16 = jnp.bfloat16


def swap(value, axis):
    return lax.ppermute(value, axis, [(0, 1), (1, 0)])


def shift(value, amount):
    size = lax.axis_size("line")
    return lax.ppermute(value, "line", [(i, (i + amount) % size) for i in range(size)])


def part_of(value, start, size, axis):
    return lax.dynamic_slice_in_dim(value, start, size, axis, allow_negative_indices=False)


def relative(value, axis, index):
    return jnp.where(index == 0, value, jnp.flip(value, axis))


def in_hbm(value):
    return pltpu.with_memory_space_constraint(value, pltpu.HBM)


def attend_kernel(length_ref, query_ref, cache_ref, out_ref):
    rows, depth = out_ref.shape[0], out_ref.shape[2]
    scores = [
        jnp.dot(query_ref[i], cache_ref[i], preferred_element_type=F32) for i in range(rows)
    ]
    positions = lax.broadcasted_iota(jnp.int32, scores[0].shape, 1)
    probs = []
    for i in range(rows):
        in_range = positions < length_ref[pl.program_id(0) * rows + i]
        masked = jnp.where(in_range, scores[i] * SOFTMAX_SCALE, MASK_VALUE)
        row_max = jnp.max(masked, axis=1, keepdims=True)
        exp_scores = jnp.where(in_range, jnp.exp(masked - row_max), 0.0)
        probs.append((exp_scores / jnp.sum(exp_scores, axis=1, keepdims=True)).astype(BF16))
    latent = [
        lax.dot_general(
            probs[i], cache_ref[i, :depth, :], (((1,), (1,)), ((), ())), preferred_element_type=F32
        )
        for i in range(rows)
    ]
    for i in range(rows):
        out_ref[i] = latent[i].astype(BF16)


def attend(queries, latent_cache, cache_len, value_up):
    rows, heads, depth = queries.shape
    positions = latent_cache.shape[1]
    tile = 8
    latent_out = pl.pallas_call(
        attend_kernel,
        grid_spec=pltpu.PrefetchScalarGridSpec(
            num_scalar_prefetch=1,
            grid=(rows // tile,),
            in_specs=[
                pl.BlockSpec((tile, heads, depth), lambda r, length: (r, 0, 0)),
                pl.BlockSpec((tile, depth, positions), lambda r, length: (r, 0, 0)),
            ],
            out_specs=pl.BlockSpec((tile, heads, LAT), lambda r, length: (r, 0, 0)),
        ),
        out_shape=jax.ShapeDtypeStruct((rows, heads, LAT), BF16),
        compiler_params=pltpu.CompilerParams(vmem_limit_bytes=16 * MIB),
        cost_estimate=pl.CostEstimate(
            flops=2 * rows * heads * positions * (depth + LAT),
            bytes_accessed=2 * rows * (heads * (depth + LAT) + positions * depth),
            transcendentals=rows * heads * positions,
        ),
    )(cache_len, in_hbm(queries), in_hbm(latent_cache.transpose(0, 2, 1)))
    heads_out = jnp.einsum("rhc,hcv->rhv", latent_out, value_up, preferred_element_type=F32)
    return heads_out.astype(BF16).reshape(rows, heads * VDIM)


def project_kernel(slots, start, first, place_ref, own_ref, sibling_ref, *refs):
    blocks, (out_ref, rows_ref, weight_ref, total_ref, arrived) = refs[:-5], refs[-5:]
    if not first:
        earlier_ref, *blocks = blocks
    count, (size, depth), width = len(slots), blocks[0].shape, own_ref.shape[0]
    tile = min(2048, depth)
    tiles = depth // tile

    def rows_copy(i, block):
        start = pl.multiple_of(place_ref[2 * i + 1] * size, size)
        return pltpu.make_async_copy(block, rows_ref.at[pl.ds(start, size)], arrived.at[i])

    def weight_copy(half, k):
        columns = pl.ds(pl.multiple_of(k * tile, tile), tile)
        source, place = ((own_ref, place_ref[2 * count]), (sibling_ref, 1 - place_ref[2 * count]))[half]
        return pltpu.make_async_copy(
            source.at[:, pl.ds(pl.multiple_of(start + k * tile, tile), tile)],
            weight_ref.at[pl.ds(pl.multiple_of(place * width, 16), width), columns],
            arrived.at[count + half * tiles + k],
        )

    for i, slot in enumerate(slots):
        if len(slot) == 1:
            rows_copy(i, blocks[slot[0]]).start()
            continue
        from_left = place_ref[2 * i] == 1

        @pl.when(from_left)
        def _():
            rows_copy(i, blocks[slot[0]]).start()

        @pl.when(jnp.logical_not(from_left))
        def _():
            rows_copy(i, blocks[slot[1]]).start()

    for k in range(tiles):
        for half in range(2):
            weight_copy(half, k).start()
    total_ref[...] = jnp.zeros_like(total_ref)
    for i in range(count):
        rows_copy(i, blocks[0]).wait()

    def step(k, _):
        columns = pl.ds(pl.multiple_of(k * tile, tile), tile)
        for half in range(2):
            weight_copy(half, k).wait()
        total_ref[...] += lax.dot_general(
            weight_ref[:, columns],
            rows_ref[:, columns],
            (((1,), (1,)), ((), ())),
            preferred_element_type=F32,
        )
        return 0

    lax.fori_loop(0, tiles, step, 0)
    total = total_ref[...].T
    if not first:
        total = total + earlier_ref[...]
    out_ref[...] = total.astype(out_ref.dtype)


def project(place, slots, blocks, own, sibling, start, earlier, dtype):
    vmem = pl.BlockSpec(memory_space=pltpu.VMEM)
    first = earlier is None
    count, (size, depth) = len(slots), blocks[0].shape
    width = own.shape[0]
    anywhere = pl.BlockSpec(memory_space=pl.ANY)
    return pl.pallas_call(
        functools.partial(project_kernel, slots, start, first),
        in_specs=[pl.BlockSpec(memory_space=pltpu.SMEM)]
        + [anywhere] * 2
        + ([] if first else [vmem])
        + [anywhere] * len(blocks),
        out_specs=vmem,
        out_shape=jax.ShapeDtypeStruct((count * size, 2 * width), dtype),
        scratch_shapes=[
            pltpu.VMEM((count * size, depth), BF16),
            pltpu.VMEM((2 * width, depth), BF16),
            pltpu.VMEM((2 * width, count * size), F32),
            pltpu.SemaphoreType.DMA((count + 2 * (depth // min(2048, depth)),)),
        ],
        compiler_params=pltpu.CompilerParams(vmem_limit_bytes=16 * MIB),
        cost_estimate=pl.CostEstimate(
            flops=4 * count * size * depth * width,
            bytes_accessed=2 * depth * (2 * width + count * size),
            transcendentals=0,
        ),
    )(place, in_hbm(own), in_hbm(sibling), *([] if first else [earlier]), *blocks)


def hidden_kernel(layout, first, last, place_ref, *refs):
    total, count = 1 + max(copy[0] for unit in layout for copy in unit), len(layout)
    pieces, (gate_ref, up_ref, *rest) = refs[:total], refs[total:]
    if not first:
        gate_in, up_in, *rest = rest
    if last:
        weight_ref, hidden_ref, *rest = rest
    else:
        gate_out, up_out, *rest = rest
    rows_ref, gate_rows, up_rows, *rest, arrived, fetched, summed = rest
    sums = rest
    size, width = pieces[0].shape[1:]
    depth, columns = 2 * width, gate_ref.shape[1]
    tile = min(512, columns)
    copies = []
    for start, unit in enumerate(layout):
        for piece, entry, row, side in unit:
            column = pl.multiple_of(start * depth + (place_ref[count] + side) % 2 * width, 128)
            copies.append(
                pltpu.make_async_copy(
                    pieces[piece].at[entry],
                    rows_ref.at[pl.ds(row * size, size), pl.ds(column, width)],
                    arrived.at[len(copies)],
                )
            )

    def weight_copies(n, matrix):
        part = pl.ds(pl.multiple_of(n * tile, tile), tile)
        source, target = ((gate_ref, gate_rows), (up_ref, up_rows))[matrix]
        return [
            pltpu.make_async_copy(
                source.at[pl.ds(pl.multiple_of(place_ref[i] * depth + j * width, width), width), part],
                target.at[pl.ds(i * depth + j * width, width), part],
                fetched.at[n, matrix, i, j],
            )
            for i in range(count)
            for j in range(2)
        ]

    def sum_copy(n, matrix, out):
        part = pl.ds(pl.multiple_of(n * tile, tile), tile)
        here = sums[matrix].at[:, part]
        if out:
            there = (gate_out, up_out)[matrix].at[:, part]
            return pltpu.make_async_copy(here, there, summed.at[n, matrix, 1])
        there = (gate_in, up_in)[matrix].at[:, part]
        return pltpu.make_async_copy(there, here, summed.at[n, matrix, 0])

    steps = columns // tile
    for copy in copies:
        copy.start()
    for n in range(steps):
        for matrix in range(2):
            for copy in weight_copies(n, matrix):
                copy.start()
            if not first:
                sum_copy(n, matrix, False).start()
    for copy in copies:
        copy.wait()

    def step(n, _):
        inner = min(256, tile)
        for matrix in range(2):
            for copy in weight_copies(n, matrix):
                copy.wait()
            if not first:
                sum_copy(n, matrix, False).wait()
            for start in range(0, tile, inner):
                part = pl.ds(pl.multiple_of(n * tile + start, inner), inner)
                value = jnp.dot(
                    rows_ref[...], (gate_rows, up_rows)[matrix][:, part], preferred_element_type=F32
                )
                if not first:
                    value += sums[matrix][:, part]
                if last and matrix:
                    gate = sums[0][:, part]
                    hidden_ref[:, part] = (
                        weight_ref[:, :1] * (gate / (1.0 + jnp.exp(-gate))) * value
                    ).astype(hidden_ref.dtype)
                else:
                    sums[matrix][:, part] = value
            if not last:
                sum_copy(n, matrix, True).start()
        return 0

    lax.fori_loop(0, steps, step, 0)
    if not last:
        for n in range(steps):
            for matrix in range(2):
                sum_copy(n, matrix, True).wait()


def hidden_part(units, places, pieces, w_gate, w_up, sums=None, weight=None):
    first, last = sums is None, weight is not None
    size, width = pieces[0].shape[1:]
    rows, columns, depth = 4 * size, w_gate.shape[1], 2 * width
    layout, piece = [], 0
    for unit in units:
        layout.append([])
        for core in range(2):
            for place_of in unit:
                for at, (sect, near) in enumerate(place_of):
                    layout[-1].append((piece, at, core * 2 + sect, near))
                piece += 1
    anywhere, vmem = pl.BlockSpec(memory_space=pl.ANY), pl.BlockSpec(memory_space=pltpu.VMEM)
    in_specs = [pl.BlockSpec(memory_space=pltpu.SMEM)] + [anywhere] * (len(pieces) + 2)
    operands = list(pieces) + [in_hbm(w_gate), in_hbm(w_up)]
    if not first:
        in_specs += [anywhere] * 2
        operands += list(sums)
    if last:
        in_specs += [vmem]
        operands += [weight]
        out_shape, out_specs = jax.ShapeDtypeStruct((rows, columns), BF16), vmem
    else:
        out_shape = [jax.ShapeDtypeStruct((rows, columns), F32)] * 2
        out_specs = [anywhere] * 2
    steps = columns // min(512, columns)
    return pl.pallas_call(
        functools.partial(hidden_kernel, layout, first, last),
        in_specs=in_specs,
        out_specs=out_specs,
        out_shape=out_shape,
        scratch_shapes=[pltpu.VMEM((rows, len(units) * depth), BF16)]
        + [pltpu.VMEM((len(units) * depth, columns), BF16)] * 2
        + [pltpu.VMEM((rows, columns), F32)] * 2
        + [
            pltpu.SemaphoreType.DMA((sum(len(unit) for unit in layout),)),
            pltpu.SemaphoreType.DMA((steps, 2, len(units), 2)),
            pltpu.SemaphoreType.DMA((steps, 2, 2)),
        ],
        compiler_params=pltpu.CompilerParams(vmem_limit_bytes=(12 + 10 * len(units)) * MIB),
        cost_estimate=pl.CostEstimate(
            flops=4 * rows * len(units) * depth * columns,
            bytes_accessed=4 * len(units) * depth * columns,
            transcendentals=rows * columns,
        ),
    )(places, *operands)


def add(one, other):
    return (one.astype(F32) + other.astype(F32)).astype(BF16)


def on_device(
    queries,
    latent_cache,
    cache_len,
    value_up,
    out_proj,
    residual,
    w_gate,
    w_up,
    w_down,
    route_ids,
    route_weights,
):
    line = lax.axis_size("line")
    tp = lax.axis_size("tp")
    sect, at, side, core = (lax.axis_index(name) for name in ("sect", "line", "side", "core"))
    block = queries.shape[0]
    row_total, width = residual.shape
    chip_width = 2 * width
    shifts = list(range(line))

    own_proj = out_proj.T
    sibling_proj = swap(own_proj, "core")
    residual_rows = lax.dynamic_slice_in_dim(
        residual.reshape(line, 2, 2, block, width), sect * (line // 2), line // 2, 0
    )
    mine = lax.dynamic_index_in_dim(residual_rows, core, 2, keepdims=False)
    other = swap(lax.dynamic_index_in_dim(residual_rows, 1 - core, 2, keepdims=False), "core")
    residual_rows = jnp.where(
        core == 0, jnp.concatenate([mine, other], axis=3), jnp.concatenate([other, mine], axis=3)
    ).reshape(-1, chip_width)

    heads = attend(queries, latent_cache, cache_len, value_up)
    weight = jnp.sum(jnp.where(route_ids == lax.axis_index(GRP), route_weights, 0.0), axis=1)
    weight = weight.reshape(2, line // 2, 2, 2, block).transpose(3, 0, 1, 2, 4)
    weight = relative(relative(weight, 0, core), 1, sect).reshape(row_total, 1)
    weight = jnp.broadcast_to(weight, (row_total, 128))
    holders = [range(line)] + [
        value for k in shifts[1:] for value in (range(k, line), range(line - k))
    ]
    slots, place = [], []
    for k in shifts:
        slot = (2 * k - 1, 2 * (line - k)) if k else (0,)
        for y in range(2):
            slots.append(tuple(i + y * len(holders) for i in slot))
            place += [at >= k, 2 * ((at - k) % line) + (side + y) % 2]
    place = jnp.stack([jnp.asarray(value, jnp.int32) for value in place + [core]])
    half, back = line // 2, line - 1
    groups = ([0], [back], [1, half])
    group_places = [
        jnp.stack([(at - k) % line for k in group] + [side]).astype(jnp.int32) for group in groups
    ]
    index = dict(
        own_sect=sect,
        other_sect=1 - sect,
        own_side=side * chip_width,
        other_side=(1 - side) * chip_width,
        upper=at >= half,
        near_core=core == 0,
        share=lax.axis_index("tp"),
        columns=[(at + k) % line * 2 * chip_width for k in shifts],
    )
    length, partial, blocks = heads.shape[1] // 2, None, []
    for part in range(2):
        own = heads[:, part * length : (part + 1) * length]
        if part:
            own, weight, residual_rows, place, group_places, index = lax.optimization_barrier(
                (own, weight, residual_rows, place, group_places, index)
            )
        rights, lefts = [own], [own]
        for k in shifts[1:]:
            if k == 3 and not part:
                rights[-1], sibling_proj = lax.optimization_barrier((rights[-1], sibling_proj))
            right = [(i, i + 1) for i in range(k - 1, line - 1)]
            left = [(i, i - 1) for i in range(1, line - k + 1)]
            rights.append(lax.ppermute(rights[-1], "line", right))
            lefts.append(lax.ppermute(lefts[-1], "line", left))
        near = [own] + [value for pair in zip(rights[1:], lefts[1:]) for value in pair]
        far = [
            lax.ppermute(
                value, ("line", "side"), [(2 * i + y, 2 * i + 1 - y) for i in held for y in range(2)]
            )
            for value, held in zip(near, holders)
        ]
        blocks.append(near + far)
    for part in range(2):
        partial = project(
            place,
            slots,
            blocks[part],
            own_proj,
            sibling_proj,
            part * length,
            partial,
            BF16 if part and tp == 1 else F32,
        )
    if tp > 1:
        partial = lax.psum(partial, "tp").astype(BF16)
    partial = partial.reshape(2, -1, chip_width)
    kept = part_of(partial, index["own_sect"], 1, 0)[0]
    given = part_of(partial, index["other_sect"], 1, 0)[0]
    attention = kept.astype(F32) + swap(given, "sect").astype(F32)
    own_rows = (residual_rows.astype(F32) + attention).astype(BF16)

    got = {k: shift(own_rows, k) if k else own_rows for k in shifts if k != line // 2}
    right = lax.ppermute(got[1], "line", [(i, i + 1) for i in range(1, line - 1)])
    left = lax.ppermute(got[line - 1], "line", [(i, i - 1) for i in range(1, line - 1)])
    got[line // 2] = jnp.where(index["upper"], right, left)
    pairs, opposites = {}, {}
    for k in (0, back, 1, half):
        first, second = ("sect", "side") if k % 2 == 0 else ("side", "sect")
        pairs[k] = jnp.stack([got[k], swap(got[k], first)])
        opposites[k] = swap(pairs[k], second)
    layout = [
        [[(0, 0), (1, 0)], [(0, 1), (1, 1)]] if k % 2 == 0 else [[(0, 0), (0, 1)], [(1, 0), (1, 1)]]
        for k in shifts
    ]
    sums = None
    for group, places in zip(groups, group_places):
        if group == [back]:
            for k in (back, 1, half):
                opposites[k], _ = lax.optimization_barrier((opposites[k], sums))
        sums = hidden_part(
            [layout[k] for k in group],
            places,
            [
                piece
                for k in group
                for piece in (
                    pairs[k], opposites[k], swap(pairs[k], "core"), swap(opposites[k], "core")
                )
            ],
            w_gate[0],
            w_up[0],
            sums,
            weight if half in group else None,
        )
    hidden = sums

    def own_side(value):
        return part_of(value, index["own_side"], chip_width, value.ndim - 1)

    def other_side(value):
        return part_of(value, index["other_side"], chip_width, value.ndim - 1)

    count = row_total // 2
    send, keep = (
        jnp.dot(rows, w_down[0], preferred_element_type=F32) for rows in (hidden[count:], hidden[:count])
    )
    if tp > 1:
        send, keep = (lax.psum(v, "tp") for v in (send, keep))
    send, keep = send.astype(BF16), keep.astype(BF16)

    def columns_to(value, k):
        return part_of(value, index["columns"][k], 2 * chip_width, 1)

    total, held = own_rows.astype(F32), None
    for group in ((half, 1), (back, 0)):
        arrived = swap(jnp.stack([columns_to(send, k) for k in group]), "core")
        if held is not None:
            arrived, held = lax.optimization_barrier((arrived, held))
        for k, arrival in zip(group, arrived):
            part = add(columns_to(keep, k), arrival).reshape(2, -1, 2 * chip_width)
            if k % 2 == 0:
                part = add(part[0], swap(part[1], "sect"))
                held = part
                part = add(own_side(part), swap(other_side(part), "side"))
            else:
                part = add(own_side(part), swap(other_side(part), "side"))
                part = add(part[0], swap(part[1], "sect"))
            total = total + (shift(part, k) if k else part).astype(F32)
    total = total.astype(BF16)

    mine = jnp.where(index["near_core"], total[:, :width], total[:, width:])
    other = swap(jnp.where(index["near_core"], total[:, width:], total[:, :width]), "core")
    out = jnp.where(index["near_core"], jnp.stack([mine, other]), jnp.stack([other, mine]))
    out = out.reshape(2, -1, block, width).transpose(1, 0, 2, 3).reshape(-1, width)
    share = out.shape[0] // tp
    return part_of(out, index["share"] * share, share, 0) if tp > 1 else out


def solution(mesh):
    sizes = dict(mesh.shape)
    fine = Mesh(
        mesh.devices.reshape(sizes["sect"], sizes["grp"] // 4, 2, 2, sizes["tp"]),
        ("sect", "line", "side", "core", "tp"),
    )
    return jax.shard_map(
        on_device,
        mesh=fine,
        in_specs=(
            P(GRP, HID, None),
            P(GRP, None, None),
            P(GRP),
            P(HID, None, None),
            P(HID, GRP),
            P(None, GRP),
            P(GRP, None, HID),
            P(GRP, None, HID),
            P(GRP, HID, None),
            P(),
            P(),
        ),
        out_specs=P(HID, GRP),
        check_vma=False,
    )
```

```python
import functools

import jax
import jax.numpy as jnp
from jax import lax
from jax.experimental import pallas as pl
from jax.experimental.pallas import tpu as pltpu
from jax.sharding import Mesh
from jax.sharding import PartitionSpec as P

LAT = 512
VDIM = 128
SOFTMAX_SCALE = 0.0721688
MASK_VALUE = -1e30
MIB = 1024 * 1024

GRP = ("line", "side", "core")
HID = ("sect", "tp")
F32 = jnp.float32
BF16 = jnp.bfloat16


def swap(value, axis):
    return lax.ppermute(value, axis, [(0, 1), (1, 0)])


def shift(value, amount):
    size = lax.axis_size("line")
    return lax.ppermute(value, "line", [(i, (i + amount) % size) for i in range(size)])


def part_of(value, start, size, axis):
    return lax.dynamic_slice_in_dim(value, start, size, axis, allow_negative_indices=False)


def relative(value, axis, index):
    return jnp.where(index == 0, value, jnp.flip(value, axis))


def in_hbm(value):
    return pltpu.with_memory_space_constraint(value, pltpu.HBM)


def attend_kernel(length_ref, query_ref, cache_ref, out_ref):
    rows, depth = out_ref.shape[0], out_ref.shape[2]
    scores = [
        jnp.dot(query_ref[i], cache_ref[i], preferred_element_type=F32) for i in range(rows)
    ]
    positions = lax.broadcasted_iota(jnp.int32, scores[0].shape, 1)
    probs = []
    for i in range(rows):
        in_range = positions < length_ref[pl.program_id(0) * rows + i]
        masked = jnp.where(in_range, scores[i] * SOFTMAX_SCALE, MASK_VALUE)
        row_max = jnp.max(masked, axis=1, keepdims=True)
        exp_scores = jnp.where(in_range, jnp.exp(masked - row_max), 0.0)
        probs.append((exp_scores / jnp.sum(exp_scores, axis=1, keepdims=True)).astype(BF16))
    latent = [
        lax.dot_general(
            probs[i], cache_ref[i, :depth, :], (((1,), (1,)), ((), ())), preferred_element_type=F32
        )
        for i in range(rows)
    ]
    for i in range(rows):
        out_ref[i] = latent[i].astype(BF16)


def attend(queries, latent_cache, cache_len, value_up):
    rows, heads, depth = queries.shape
    positions = latent_cache.shape[1]
    tile = 8
    latent_out = pl.pallas_call(
        attend_kernel,
        grid_spec=pltpu.PrefetchScalarGridSpec(
            num_scalar_prefetch=1,
            grid=(rows // tile,),
            in_specs=[
                pl.BlockSpec((tile, heads, depth), lambda r, length: (r, 0, 0)),
                pl.BlockSpec((tile, depth, positions), lambda r, length: (r, 0, 0)),
            ],
            out_specs=pl.BlockSpec((tile, heads, LAT), lambda r, length: (r, 0, 0)),
        ),
        out_shape=jax.ShapeDtypeStruct((rows, heads, LAT), BF16),
        compiler_params=pltpu.CompilerParams(vmem_limit_bytes=16 * MIB),
        cost_estimate=pl.CostEstimate(
            flops=2 * rows * heads * positions * (depth + LAT),
            bytes_accessed=2 * rows * (heads * (depth + LAT) + positions * depth),
            transcendentals=rows * heads * positions,
        ),
    )(cache_len, in_hbm(queries), in_hbm(latent_cache.transpose(0, 2, 1)))
    heads_out = jnp.einsum("rhc,hcv->rhv", latent_out, value_up, preferred_element_type=F32)
    return heads_out.astype(BF16).reshape(rows, heads * VDIM)


def project_kernel(slots, start, first, place_ref, own_ref, sibling_ref, *refs):
    blocks, (out_ref, rows_ref, weight_ref, total_ref, arrived) = refs[:-5], refs[-5:]
    if not first:
        earlier_ref, *blocks = blocks
    count, (size, depth), width = len(slots), blocks[0].shape, own_ref.shape[0]
    tile = min(2048, depth)
    tiles = depth // tile

    def rows_copy(i, block):
        start = pl.multiple_of(place_ref[2 * i + 1] * size, size)
        return pltpu.make_async_copy(block, rows_ref.at[pl.ds(start, size)], arrived.at[i])

    def weight_copy(half, k):
        columns = pl.ds(pl.multiple_of(k * tile, tile), tile)
        source, place = ((own_ref, place_ref[2 * count]), (sibling_ref, 1 - place_ref[2 * count]))[half]
        return pltpu.make_async_copy(
            source.at[:, pl.ds(pl.multiple_of(start + k * tile, tile), tile)],
            weight_ref.at[pl.ds(pl.multiple_of(place * width, 16), width), columns],
            arrived.at[count + half * tiles + k],
        )

    for i, slot in enumerate(slots):
        if len(slot) == 1:
            rows_copy(i, blocks[slot[0]]).start()
            continue
        from_left = place_ref[2 * i] == 1

        @pl.when(from_left)
        def _():
            rows_copy(i, blocks[slot[0]]).start()

        @pl.when(jnp.logical_not(from_left))
        def _():
            rows_copy(i, blocks[slot[1]]).start()

    for k in range(tiles):
        for half in range(2):
            weight_copy(half, k).start()
    total_ref[...] = jnp.zeros_like(total_ref)
    for i in range(count):
        rows_copy(i, blocks[0]).wait()

    def step(k, _):
        columns = pl.ds(pl.multiple_of(k * tile, tile), tile)
        for half in range(2):
            weight_copy(half, k).wait()
        total_ref[...] += lax.dot_general(
            weight_ref[:, columns],
            rows_ref[:, columns],
            (((1,), (1,)), ((), ())),
            preferred_element_type=F32,
        )
        return 0

    lax.fori_loop(0, tiles, step, 0)
    total = total_ref[...].T
    if not first:
        total = total + earlier_ref[...]
    out_ref[...] = total.astype(out_ref.dtype)


def project(place, slots, blocks, own, sibling, start, earlier, dtype):
    vmem = pl.BlockSpec(memory_space=pltpu.VMEM)
    first = earlier is None
    count, (size, depth) = len(slots), blocks[0].shape
    width = own.shape[0]
    anywhere = pl.BlockSpec(memory_space=pl.ANY)
    return pl.pallas_call(
        functools.partial(project_kernel, slots, start, first),
        in_specs=[pl.BlockSpec(memory_space=pltpu.SMEM)]
        + [anywhere] * 2
        + ([] if first else [vmem])
        + [anywhere] * len(blocks),
        out_specs=vmem,
        out_shape=jax.ShapeDtypeStruct((count * size, 2 * width), dtype),
        scratch_shapes=[
            pltpu.VMEM((count * size, depth), BF16),
            pltpu.VMEM((2 * width, depth), BF16),
            pltpu.VMEM((2 * width, count * size), F32),
            pltpu.SemaphoreType.DMA((count + 2 * (depth // min(2048, depth)),)),
        ],
        compiler_params=pltpu.CompilerParams(vmem_limit_bytes=16 * MIB),
        cost_estimate=pl.CostEstimate(
            flops=4 * count * size * depth * width,
            bytes_accessed=2 * depth * (2 * width + count * size),
            transcendentals=0,
        ),
    )(place, in_hbm(own), in_hbm(sibling), *([] if first else [earlier]), *blocks)


def hidden_kernel(layout, first, last, place_ref, *refs):
    total, count = 1 + max(copy[0] for unit in layout for copy in unit), len(layout)
    pieces, (gate_ref, up_ref, *rest) = refs[:total], refs[total:]
    if not first:
        gate_in, up_in, *rest = rest
    if last:
        weight_ref, down_ref, hidden_ref, send_ref, *rest, down_rows, down_fetched = rest
    else:
        gate_out, up_out, *rest = rest
    rows_ref, gate_rows, up_rows, *sums, arrived, fetched, summed = rest
    size, width = pieces[0].shape[1:]
    depth, columns = 2 * width, gate_ref.shape[1]
    tile = min(512, columns)
    copies = []
    for start, unit in enumerate(layout):
        for piece, entry, row, side in unit:
            column = pl.multiple_of(start * depth + (place_ref[count] + side) % 2 * width, 128)
            copies.append(
                pltpu.make_async_copy(
                    pieces[piece].at[entry],
                    rows_ref.at[pl.ds(row * size, size), pl.ds(column, width)],
                    arrived.at[len(copies)],
                )
            )

    def weight_copies(n, matrix):
        part = pl.ds(pl.multiple_of(n * tile, tile), tile)
        source, target = ((gate_ref, gate_rows), (up_ref, up_rows))[matrix]
        return [
            pltpu.make_async_copy(
                source.at[pl.ds(pl.multiple_of(place_ref[i] * depth + j * width, width), width), part],
                target.at[pl.ds(i * depth + j * width, width), part],
                fetched.at[n, matrix, i, j],
            )
            for i in range(count)
            for j in range(2)
        ]

    def sum_copy(n, matrix, out):
        part = pl.ds(pl.multiple_of(n * tile, tile), tile)
        here = sums[matrix].at[:, part]
        if out:
            there = (gate_out, up_out)[matrix].at[:, part]
            return pltpu.make_async_copy(here, there, summed.at[n, matrix, 1])
        there = (gate_in, up_in)[matrix].at[:, part]
        return pltpu.make_async_copy(there, here, summed.at[n, matrix, 0])

    steps = columns // tile
    for copy in copies:
        copy.start()
    for n in range(steps):
        for matrix in range(2):
            for copy in weight_copies(n, matrix):
                copy.start()
            if not first:
                sum_copy(n, matrix, False).start()
    if last:
        down = down_copies(place_ref, count + 1, send_ref.shape[0], down_ref, down_rows, down_fetched)
        for copy in down:
            copy.start()
    for copy in copies:
        copy.wait()

    def step(n, _):
        inner = min(256, tile)
        for matrix in range(2):
            for copy in weight_copies(n, matrix):
                copy.wait()
            if not first:
                sum_copy(n, matrix, False).wait()
            for start in range(0, tile, inner):
                part = pl.ds(pl.multiple_of(n * tile + start, inner), inner)
                value = jnp.dot(
                    rows_ref[...], (gate_rows, up_rows)[matrix][:, part], preferred_element_type=F32
                )
                if not first:
                    value += sums[matrix][:, part]
                if last and matrix:
                    gate = sums[0][:, part]
                    hidden_ref[:, part] = (
                        weight_ref[:, :1] * (gate / (1.0 + jnp.exp(-gate))) * value
                    ).astype(hidden_ref.dtype)
                else:
                    sums[matrix][:, part] = value
            if not last:
                sum_copy(n, matrix, True).start()
        return 0

    lax.fori_loop(0, steps, step, 0)
    if last:
        for copy in down:
            copy.wait()
        rows = send_ref.shape[1]
        for i in range(send_ref.shape[0]):
            down_products(hidden_ref[rows:], down_rows, i, send_ref)
    else:
        for n in range(steps):
            for matrix in range(2):
                sum_copy(n, matrix, True).wait()


def down_copies(place_ref, start, count, source_ref, target_ref, arrived):
    depth, width = source_ref.shape[0], target_ref.shape[1] // count
    half = depth // 2
    return [
        pltpu.make_async_copy(
            source_ref.at[
                pl.ds(j * half, half),
                pl.ds(pl.multiple_of(place_ref[start + i] * width, 128), width),
            ],
            target_ref.at[pl.ds(j * half, half), pl.ds(i * width, width)],
            arrived.at[2 * i + j],
        )
        for i in range(count)
        for j in range(2)
    ]


def down_products(rows, weight_ref, i, out_ref):
    width, tile = out_ref.shape[2], 256

    def step(n, _):
        columns = pl.ds(pl.multiple_of(i * width + n * tile, tile), tile)
        out_ref[i, :, pl.ds(pl.multiple_of(n * tile, tile), tile)] = jnp.dot(
            rows, weight_ref[:, columns], preferred_element_type=F32
        ).astype(out_ref.dtype)
        return 0

    lax.fori_loop(0, width // tile, step, 0)


def down_kernel(halves, place_ref, hidden_ref, weight_ref, *refs):
    outs, (weight_rows, arrived) = refs[:-2], refs[-2:]
    amount, rows, _ = outs[0].shape
    copies = down_copies(place_ref, 0, amount, weight_ref, weight_rows, arrived)
    for copy in copies:
        copy.start()
    for i in range(amount):
        for copy in copies[2 * i : 2 * i + 2]:
            copy.wait()
        for half, out_ref in zip(halves, outs):
            down_products(hidden_ref[half * rows : (half + 1) * rows], weight_rows, i, out_ref)


def down_part(places, halves, hidden, w_down, width):
    rows, units = hidden.shape[0] // 2, hidden.shape[1]
    vmem = pl.BlockSpec(memory_space=pltpu.VMEM)
    return pl.pallas_call(
        functools.partial(down_kernel, halves),
        in_specs=[
            pl.BlockSpec(memory_space=pltpu.SMEM),
            vmem,
            pl.BlockSpec(memory_space=pl.ANY),
        ],
        out_specs=[vmem] * len(halves),
        out_shape=[jax.ShapeDtypeStruct((2, rows, width), BF16)] * len(halves),
        scratch_shapes=[pltpu.VMEM((units, 2 * width), BF16), pltpu.SemaphoreType.DMA((4,))],
        compiler_params=pltpu.CompilerParams(vmem_limit_bytes=18 * MIB),
        cost_estimate=pl.CostEstimate(
            flops=4 * len(halves) * rows * units * width,
            bytes_accessed=4 * units * width,
            transcendentals=0,
        ),
    )(places, hidden, in_hbm(w_down))


def hidden_part(units, places, pieces, w_gate, w_up, sums=None, weight=None, w_down=None):
    first, last = sums is None, weight is not None
    size, width = pieces[0].shape[1:]
    rows, columns, depth = 4 * size, w_gate.shape[1], 2 * width
    layout, piece = [], 0
    for unit in units:
        layout.append([])
        for core in range(2):
            for place_of in unit:
                for at, (sect, near) in enumerate(place_of):
                    layout[-1].append((piece, at, core * 2 + sect, near))
                piece += 1
    anywhere, vmem = pl.BlockSpec(memory_space=pl.ANY), pl.BlockSpec(memory_space=pltpu.VMEM)
    in_specs = [pl.BlockSpec(memory_space=pltpu.SMEM)] + [anywhere] * (len(pieces) + 2)
    operands = list(pieces) + [in_hbm(w_gate), in_hbm(w_up)]
    if not first:
        in_specs += [anywhere] * 2
        operands += list(sums)
    scratch = []
    if last:
        in_specs += [vmem, anywhere]
        operands += [weight, in_hbm(w_down)]
        out_shape = [
            jax.ShapeDtypeStruct((rows, columns), BF16),
            jax.ShapeDtypeStruct((2, rows // 2, depth), BF16),
        ]
        out_specs = [vmem] * 2
        scratch = [pltpu.VMEM((columns, 2 * depth), BF16), pltpu.SemaphoreType.DMA((4,))]
    else:
        out_shape = [jax.ShapeDtypeStruct((rows, columns), F32)] * 2
        out_specs = [anywhere] * 2
    steps = columns // min(512, columns)
    return pl.pallas_call(
        functools.partial(hidden_kernel, layout, first, last),
        in_specs=in_specs,
        out_specs=out_specs,
        out_shape=out_shape,
        scratch_shapes=[pltpu.VMEM((rows, len(units) * depth), BF16)]
        + [pltpu.VMEM((len(units) * depth, columns), BF16)] * 2
        + [pltpu.VMEM((rows, columns), F32)] * 2
        + [
            pltpu.SemaphoreType.DMA((sum(len(unit) for unit in layout),)),
            pltpu.SemaphoreType.DMA((steps, 2, len(units), 2)),
            pltpu.SemaphoreType.DMA((steps, 2, 2)),
        ]
        + scratch,
        compiler_params=pltpu.CompilerParams(
            vmem_limit_bytes=(12 + 10 * len(units) + 10 * last) * MIB
        ),
        cost_estimate=pl.CostEstimate(
            flops=4 * rows * len(units) * depth * columns,
            bytes_accessed=4 * len(units) * depth * columns,
            transcendentals=rows * columns,
        ),
    )(places, *operands)


def add(one, other):
    return (one.astype(F32) + other.astype(F32)).astype(BF16)


def on_device(
    queries,
    latent_cache,
    cache_len,
    value_up,
    out_proj,
    residual,
    w_gate,
    w_up,
    w_down,
    route_ids,
    route_weights,
):
    line = lax.axis_size("line")
    tp = lax.axis_size("tp")
    sect, at, side, core = (lax.axis_index(name) for name in ("sect", "line", "side", "core"))
    block = queries.shape[0]
    row_total, width = residual.shape
    chip_width = 2 * width
    shifts = list(range(line))

    own_proj = out_proj.T
    sibling_proj = swap(own_proj, "core")
    residual_rows = lax.dynamic_slice_in_dim(
        residual.reshape(line, 2, 2, block, width), sect * (line // 2), line // 2, 0
    )
    mine = lax.dynamic_index_in_dim(residual_rows, core, 2, keepdims=False)
    other = swap(lax.dynamic_index_in_dim(residual_rows, 1 - core, 2, keepdims=False), "core")
    residual_rows = jnp.where(
        core == 0, jnp.concatenate([mine, other], axis=3), jnp.concatenate([other, mine], axis=3)
    ).reshape(-1, chip_width)

    heads = attend(queries, latent_cache, cache_len, value_up)
    weight = jnp.sum(jnp.where(route_ids == lax.axis_index(GRP), route_weights, 0.0), axis=1)
    weight = weight.reshape(2, line // 2, 2, 2, block).transpose(3, 0, 1, 2, 4)
    weight = relative(relative(weight, 0, core), 1, sect).reshape(row_total, 1)
    weight = jnp.broadcast_to(weight, (row_total, 128))
    holders = [range(line)] + [
        value for k in shifts[1:] for value in (range(k, line), range(line - k))
    ]
    slots, place = [], []
    for k in shifts:
        slot = (2 * k - 1, 2 * (line - k)) if k else (0,)
        for y in range(2):
            slots.append(tuple(i + y * len(holders) for i in slot))
            place += [at >= k, 2 * ((at - k) % line) + (side + y) % 2]
    place = jnp.stack([jnp.asarray(value, jnp.int32) for value in place + [core]])
    half, back = line // 2, line - 1
    groups = ([0], [back], [1, half])
    group_places = [
        jnp.stack(
            [(at - k) % line for k in group]
            + [side]
            + ([(at + k) % line for k in (half, 1)] if half in group else [])
        ).astype(jnp.int32)
        for group in groups
    ]
    down_places = [
        jnp.stack([(at + k) % line for k in group]).astype(jnp.int32)
        for group in ((half, 1), (back, 0))
    ]
    index = dict(
        own_sect=sect,
        other_sect=1 - sect,
        own_side=side * chip_width,
        other_side=(1 - side) * chip_width,
        upper=at >= half,
        near_core=core == 0,
        share=lax.axis_index("tp"),
    )
    length, partial, blocks = heads.shape[1] // 2, None, []
    for part in range(2):
        own = heads[:, part * length : (part + 1) * length]
        if part:
            own, weight, residual_rows, place, group_places, down_places, index = (
                lax.optimization_barrier(
                    (own, weight, residual_rows, place, group_places, down_places, index)
                )
            )
        rights, lefts = [own], [own]
        for k in shifts[1:]:
            if k == 3 and not part:
                rights[-1], sibling_proj = lax.optimization_barrier((rights[-1], sibling_proj))
            right = [(i, i + 1) for i in range(k - 1, line - 1)]
            left = [(i, i - 1) for i in range(1, line - k + 1)]
            rights.append(lax.ppermute(rights[-1], "line", right))
            lefts.append(lax.ppermute(lefts[-1], "line", left))
        near = [own] + [value for pair in zip(rights[1:], lefts[1:]) for value in pair]
        far = [
            lax.ppermute(
                value, ("line", "side"), [(2 * i + y, 2 * i + 1 - y) for i in held for y in range(2)]
            )
            for value, held in zip(near, holders)
        ]
        blocks.append(near + far)
    for part in range(2):
        partial = project(
            place,
            slots,
            blocks[part],
            own_proj,
            sibling_proj,
            part * length,
            partial,
            BF16 if part and tp == 1 else F32,
        )
    if tp > 1:
        partial = lax.psum(partial, "tp").astype(BF16)
    partial = partial.reshape(2, -1, chip_width)
    kept = part_of(partial, index["own_sect"], 1, 0)[0]
    given = part_of(partial, index["other_sect"], 1, 0)[0]
    attention = kept.astype(F32) + swap(given, "sect").astype(F32)
    own_rows = (residual_rows.astype(F32) + attention).astype(BF16)

    got = {k: shift(own_rows, k) if k else own_rows for k in shifts if k != line // 2}
    right = lax.ppermute(got[1], "line", [(i, i + 1) for i in range(1, line - 1)])
    left = lax.ppermute(got[line - 1], "line", [(i, i - 1) for i in range(1, line - 1)])
    got[line // 2] = jnp.where(index["upper"], right, left)
    pairs, opposites = {}, {}
    for k in (0, back, 1, half):
        first, second = ("sect", "side") if k % 2 == 0 else ("side", "sect")
        pairs[k] = jnp.stack([got[k], swap(got[k], first)])
        opposites[k] = swap(pairs[k], second)
    layout = [
        [[(0, 0), (1, 0)], [(0, 1), (1, 1)]] if k % 2 == 0 else [[(0, 0), (0, 1)], [(1, 0), (1, 1)]]
        for k in shifts
    ]
    sums = None
    for group, places in zip(groups, group_places):
        if group == [back]:
            for k in (back, 1, half):
                opposites[k], _ = lax.optimization_barrier((opposites[k], sums))
        sums = hidden_part(
            [layout[k] for k in group],
            places,
            [
                piece
                for k in group
                for piece in (
                    pairs[k], opposites[k], swap(pairs[k], "core"), swap(opposites[k], "core")
                )
            ],
            w_gate[0],
            w_up[0],
            sums,
            weight if half in group else None,
            w_down[0] if half in group else None,
        )
    hidden, send = sums

    def own_side(value):
        return part_of(value, index["own_side"], chip_width, value.ndim - 1)

    def other_side(value):
        return part_of(value, index["other_side"], chip_width, value.ndim - 1)

    def summed(value):
        return lax.psum(value.astype(F32), "tp").astype(BF16) if tp > 1 else value

    total, held = own_rows.astype(F32), None
    for group, places in zip(((half, 1), (back, 0)), down_places):
        if held is None:
            arrived = swap(summed(send), "core")
            (keep,) = down_part(places, [0], hidden, w_down[0], 2 * chip_width)
        else:
            keep, send = down_part(places, [0, 1], hidden, w_down[0], 2 * chip_width)
            arrived, held = lax.optimization_barrier((swap(summed(send), "core"), held))
        for k, part in zip(group, add(summed(keep), arrived)):
            part = part.reshape(2, -1, 2 * chip_width)
            if k % 2 == 0:
                part = add(part[0], swap(part[1], "sect"))
                held = part
                part = add(own_side(part), swap(other_side(part), "side"))
            else:
                part = add(own_side(part), swap(other_side(part), "side"))
                part = add(part[0], swap(part[1], "sect"))
            total = total + (shift(part, k) if k else part).astype(F32)
    total = total.astype(BF16)

    mine = jnp.where(index["near_core"], total[:, :width], total[:, width:])
    other = swap(jnp.where(index["near_core"], total[:, width:], total[:, :width]), "core")
    out = jnp.where(index["near_core"], jnp.stack([mine, other]), jnp.stack([other, mine]))
    out = out.reshape(2, -1, block, width).transpose(1, 0, 2, 3).reshape(-1, width)
    share = out.shape[0] // tp
    return part_of(out, index["share"] * share, share, 0) if tp > 1 else out


def solution(mesh):
    sizes = dict(mesh.shape)
    fine = Mesh(
        mesh.devices.reshape(sizes["sect"], sizes["grp"] // 4, 2, 2, sizes["tp"]),
        ("sect", "line", "side", "core", "tp"),
    )
    return jax.shard_map(
        on_device,
        mesh=fine,
        in_specs=(
            P(GRP, HID, None),
            P(GRP, None, None),
            P(GRP),
            P(HID, None, None),
            P(HID, GRP),
            P(None, GRP),
            P(GRP, None, HID),
            P(GRP, None, HID),
            P(GRP, HID, None),
            P(),
            P(),
        ),
        out_specs=P(HID, GRP),
        check_vma=False,
    )
```

```python
import functools

import jax
import jax.numpy as jnp
from jax import lax
from jax.experimental import pallas as pl
from jax.experimental.pallas import tpu as pltpu
from jax.sharding import Mesh
from jax.sharding import PartitionSpec as P

LAT = 512
VDIM = 128
SOFTMAX_SCALE = 0.0721688
MASK_VALUE = -1e30
MIB = 1024 * 1024

GRP = ("line", "side", "core")
HID = ("sect", "tp")
F32 = jnp.float32
BF16 = jnp.bfloat16


def swap(value, axis):
    return lax.ppermute(value, axis, [(0, 1), (1, 0)])


def shift(value, amount):
    size = lax.axis_size("line")
    return lax.ppermute(value, "line", [(i, (i + amount) % size) for i in range(size)])


def part_of(value, start, size, axis):
    return lax.dynamic_slice_in_dim(value, start, size, axis, allow_negative_indices=False)


def relative(value, axis, index):
    return jnp.where(index == 0, value, jnp.flip(value, axis))


def in_hbm(value):
    return pltpu.with_memory_space_constraint(value, pltpu.HBM)


def attend_kernel(length_ref, query_ref, cache_ref, out_ref):
    rows, depth = out_ref.shape[0], out_ref.shape[2]
    scores = [
        jnp.dot(query_ref[i], cache_ref[i], preferred_element_type=F32) for i in range(rows)
    ]
    positions = lax.broadcasted_iota(jnp.int32, scores[0].shape, 1)
    probs = []
    for i in range(rows):
        in_range = positions < length_ref[pl.program_id(0) * rows + i]
        masked = jnp.where(in_range, scores[i] * SOFTMAX_SCALE, MASK_VALUE)
        row_max = jnp.max(masked, axis=1, keepdims=True)
        exp_scores = jnp.where(in_range, jnp.exp(masked - row_max), 0.0)
        probs.append((exp_scores / jnp.sum(exp_scores, axis=1, keepdims=True)).astype(BF16))
    latent = [
        lax.dot_general(
            probs[i], cache_ref[i, :depth, :], (((1,), (1,)), ((), ())), preferred_element_type=F32
        )
        for i in range(rows)
    ]
    for i in range(rows):
        out_ref[i] = latent[i].astype(BF16)


def attend(queries, latent_cache, cache_len, value_up):
    rows, heads, depth = queries.shape
    positions = latent_cache.shape[1]
    tile = 8
    latent_out = pl.pallas_call(
        attend_kernel,
        grid_spec=pltpu.PrefetchScalarGridSpec(
            num_scalar_prefetch=1,
            grid=(rows // tile,),
            in_specs=[
                pl.BlockSpec((tile, heads, depth), lambda r, length: (r, 0, 0)),
                pl.BlockSpec((tile, depth, positions), lambda r, length: (r, 0, 0)),
            ],
            out_specs=pl.BlockSpec((tile, heads, LAT), lambda r, length: (r, 0, 0)),
        ),
        out_shape=jax.ShapeDtypeStruct((rows, heads, LAT), BF16),
        compiler_params=pltpu.CompilerParams(vmem_limit_bytes=6 * MIB),
        cost_estimate=pl.CostEstimate(
            flops=2 * rows * heads * positions * (depth + LAT),
            bytes_accessed=2 * rows * (heads * (depth + LAT) + positions * depth),
            transcendentals=rows * heads * positions,
        ),
    )(cache_len, in_hbm(queries), in_hbm(latent_cache.transpose(0, 2, 1)))
    heads_out = jnp.einsum("rhc,hcv->rhv", latent_out, value_up, preferred_element_type=F32)
    return heads_out.astype(BF16).reshape(rows, heads * VDIM)


def project_kernel(slots, start, first, place_ref, own_ref, sibling_ref, *refs):
    blocks, (out_ref, rows_ref, weight_ref, total_ref, arrived) = refs[:-5], refs[-5:]
    if not first:
        earlier_ref, *blocks = blocks
    count, (size, depth), width = len(slots), blocks[0].shape, own_ref.shape[0]
    tile = min(2048, depth)
    tiles = depth // tile

    def rows_copy(i, block):
        start = pl.multiple_of(place_ref[2 * i + 1] * size, size)
        return pltpu.make_async_copy(block, rows_ref.at[pl.ds(start, size)], arrived.at[i])

    def weight_copy(half, k):
        columns = pl.ds(pl.multiple_of(k * tile, tile), tile)
        source, place = ((own_ref, place_ref[2 * count]), (sibling_ref, 1 - place_ref[2 * count]))[half]
        return pltpu.make_async_copy(
            source.at[:, pl.ds(pl.multiple_of(start + k * tile, tile), tile)],
            weight_ref.at[pl.ds(pl.multiple_of(place * width, 16), width), columns],
            arrived.at[count + half * tiles + k],
        )

    for i, slot in enumerate(slots):
        if len(slot) == 1:
            rows_copy(i, blocks[slot[0]]).start()
            continue
        from_left = place_ref[2 * i] == 1

        @pl.when(from_left)
        def _():
            rows_copy(i, blocks[slot[0]]).start()

        @pl.when(jnp.logical_not(from_left))
        def _():
            rows_copy(i, blocks[slot[1]]).start()

    for k in range(tiles):
        for half in range(2):
            weight_copy(half, k).start()
    total_ref[...] = jnp.zeros_like(total_ref)
    for i in range(count):
        rows_copy(i, blocks[0]).wait()

    def step(k, _):
        columns = pl.ds(pl.multiple_of(k * tile, tile), tile)
        for half in range(2):
            weight_copy(half, k).wait()
        total_ref[...] += lax.dot_general(
            weight_ref[:, columns],
            rows_ref[:, columns],
            (((1,), (1,)), ((), ())),
            preferred_element_type=F32,
        )
        return 0

    lax.fori_loop(0, tiles, step, 0)
    total = total_ref[...].T
    if not first:
        total = total + earlier_ref[...]
    out_ref[...] = total.astype(out_ref.dtype)


def project(place, slots, blocks, own, sibling, start, earlier, dtype):
    vmem = pl.BlockSpec(memory_space=pltpu.VMEM)
    first = earlier is None
    count, (size, depth) = len(slots), blocks[0].shape
    width = own.shape[0]
    anywhere = pl.BlockSpec(memory_space=pl.ANY)
    return pl.pallas_call(
        functools.partial(project_kernel, slots, start, first),
        in_specs=[pl.BlockSpec(memory_space=pltpu.SMEM)]
        + [anywhere] * 2
        + ([] if first else [vmem])
        + [anywhere] * len(blocks),
        out_specs=vmem,
        out_shape=jax.ShapeDtypeStruct((count * size, 2 * width), dtype),
        scratch_shapes=[
            pltpu.VMEM((count * size, depth), BF16),
            pltpu.VMEM((2 * width, depth), BF16),
            pltpu.VMEM((2 * width, count * size), F32),
            pltpu.SemaphoreType.DMA((count + 2 * (depth // min(2048, depth)),)),
        ],
        compiler_params=pltpu.CompilerParams(vmem_limit_bytes=12 * MIB),
        cost_estimate=pl.CostEstimate(
            flops=4 * count * size * depth * width,
            bytes_accessed=2 * depth * (2 * width + count * size),
            transcendentals=0,
        ),
    )(place, in_hbm(own), in_hbm(sibling), *([] if first else [earlier]), *blocks)


def hidden_kernel(layout, first, last, place_ref, *refs):
    total, count = 1 + max(copy[0] for unit in layout for copy in unit), len(layout)
    pieces, (gate_ref, up_ref, *rest) = refs[:total], refs[total:]
    if not first:
        gate_in, up_in, *rest = rest
    if last:
        weight_ref, hidden_ref, *rest = rest
    else:
        gate_out, up_out, *rest = rest
    rows_ref, gate_rows, up_rows, *rest, arrived, fetched, summed = rest
    sums = rest
    size, width = pieces[0].shape[1:]
    depth, columns = 2 * width, gate_ref.shape[1]
    tile = min(512, columns)
    copies = []
    for start, unit in enumerate(layout):
        for piece, entry, row, side in unit:
            column = pl.multiple_of(start * depth + (place_ref[count] + side) % 2 * width, 128)
            copies.append(
                pltpu.make_async_copy(
                    pieces[piece].at[entry],
                    rows_ref.at[pl.ds(row * size, size), pl.ds(column, width)],
                    arrived.at[len(copies)],
                )
            )

    def weight_copies(n, matrix):
        part = pl.ds(pl.multiple_of(n * tile, tile), tile)
        source, target = ((gate_ref, gate_rows), (up_ref, up_rows))[matrix]
        return [
            pltpu.make_async_copy(
                source.at[pl.ds(pl.multiple_of(place_ref[i] * depth + j * width, width), width), part],
                target.at[pl.ds(i * depth + j * width, width), part],
                fetched.at[n, matrix, i, j],
            )
            for i in range(count)
            for j in range(2)
        ]

    def sum_copy(n, matrix, out):
        part = pl.ds(pl.multiple_of(n * tile, tile), tile)
        here = sums[matrix].at[:, part]
        if out:
            there = (gate_out, up_out)[matrix].at[:, part]
            return pltpu.make_async_copy(here, there, summed.at[n, matrix, 1])
        there = (gate_in, up_in)[matrix].at[:, part]
        return pltpu.make_async_copy(there, here, summed.at[n, matrix, 0])

    steps = columns // tile
    for copy in copies:
        copy.start()
    for n in range(steps):
        for matrix in range(2):
            for copy in weight_copies(n, matrix):
                copy.start()
            if not first:
                sum_copy(n, matrix, False).start()
    for copy in copies:
        copy.wait()

    def step(n, _):
        inner = min(256, tile)
        for matrix in range(2):
            for copy in weight_copies(n, matrix):
                copy.wait()
            if not first:
                sum_copy(n, matrix, False).wait()
            for start in range(0, tile, inner):
                part = pl.ds(pl.multiple_of(n * tile + start, inner), inner)
                value = jnp.dot(
                    rows_ref[...], (gate_rows, up_rows)[matrix][:, part], preferred_element_type=F32
                )
                if not first:
                    value += sums[matrix][:, part]
                if last and matrix:
                    gate = sums[0][:, part]
                    hidden_ref[:, part] = (
                        weight_ref[:, :1] * (gate / (1.0 + jnp.exp(-gate))) * value
                    ).astype(hidden_ref.dtype)
                else:
                    sums[matrix][:, part] = value
            if not last:
                sum_copy(n, matrix, True).start()
        return 0

    lax.fori_loop(0, steps, step, 0)
    if not last:
        for n in range(steps):
            for matrix in range(2):
                sum_copy(n, matrix, True).wait()


def hidden_part(units, places, pieces, w_gate, w_up, sums=None, weight=None):
    first, last = sums is None, weight is not None
    size, width = pieces[0].shape[1:]
    rows, columns, depth = 4 * size, w_gate.shape[1], 2 * width
    layout, piece = [], 0
    for unit in units:
        layout.append([])
        for core in range(2):
            for place_of in unit:
                for at, (sect, near) in enumerate(place_of):
                    layout[-1].append((piece, at, core * 2 + sect, near))
                piece += 1
    anywhere, vmem = pl.BlockSpec(memory_space=pl.ANY), pl.BlockSpec(memory_space=pltpu.VMEM)
    in_specs = [pl.BlockSpec(memory_space=pltpu.SMEM)] + [anywhere] * (len(pieces) + 2)
    operands = list(pieces) + [in_hbm(w_gate), in_hbm(w_up)]
    if not first:
        in_specs += [anywhere] * 2
        operands += list(sums)
    if last:
        in_specs += [vmem]
        operands += [weight]
        out_shape, out_specs = jax.ShapeDtypeStruct((rows, columns), BF16), vmem
    else:
        out_shape = [jax.ShapeDtypeStruct((rows, columns), F32)] * 2
        out_specs = [anywhere] * 2
    steps = columns // min(512, columns)
    return pl.pallas_call(
        functools.partial(hidden_kernel, layout, first, last),
        in_specs=in_specs,
        out_specs=out_specs,
        out_shape=out_shape,
        scratch_shapes=[pltpu.VMEM((rows, len(units) * depth), BF16)]
        + [pltpu.VMEM((len(units) * depth, columns), BF16)] * 2
        + [pltpu.VMEM((rows, columns), F32)] * 2
        + [
            pltpu.SemaphoreType.DMA((sum(len(unit) for unit in layout),)),
            pltpu.SemaphoreType.DMA((steps, 2, len(units), 2)),
            pltpu.SemaphoreType.DMA((steps, 2, 2)),
        ],
        compiler_params=pltpu.CompilerParams(vmem_limit_bytes=(3 + 11 * len(units)) * MIB),
        cost_estimate=pl.CostEstimate(
            flops=4 * rows * len(units) * depth * columns,
            bytes_accessed=4 * len(units) * depth * columns,
            transcendentals=rows * columns,
        ),
    )(places, *operands)


def add(one, other):
    return (one.astype(F32) + other.astype(F32)).astype(BF16)


def on_device(
    queries,
    latent_cache,
    cache_len,
    value_up,
    out_proj,
    residual,
    w_gate,
    w_up,
    w_down,
    route_ids,
    route_weights,
):
    line = lax.axis_size("line")
    tp = lax.axis_size("tp")
    sect, at, side, core = (lax.axis_index(name) for name in ("sect", "line", "side", "core"))
    block = queries.shape[0]
    row_total, width = residual.shape
    chip_width = 2 * width
    shifts = list(range(line))

    own_proj = out_proj.T
    sibling_proj = swap(own_proj, "core")
    residual_rows = lax.dynamic_slice_in_dim(
        residual.reshape(line, 2, 2, block, width), sect * (line // 2), line // 2, 0
    )
    mine = lax.dynamic_index_in_dim(residual_rows, core, 2, keepdims=False)
    other = swap(lax.dynamic_index_in_dim(residual_rows, 1 - core, 2, keepdims=False), "core")
    residual_rows = jnp.where(
        core == 0, jnp.concatenate([mine, other], axis=3), jnp.concatenate([other, mine], axis=3)
    ).reshape(-1, chip_width)

    heads = attend(queries, latent_cache, cache_len, value_up)
    weight = jnp.sum(jnp.where(route_ids == lax.axis_index(GRP), route_weights, 0.0), axis=1)
    weight = weight.reshape(2, line // 2, 2, 2, block).transpose(3, 0, 1, 2, 4)
    weight = relative(relative(weight, 0, core), 1, sect).reshape(row_total, 1)
    weight = jnp.broadcast_to(weight, (row_total, 128))
    holders = [range(line)] + [
        value for k in shifts[1:] for value in (range(k, line), range(line - k))
    ]
    slots, place = [], []
    for k in shifts:
        slot = (2 * k - 1, 2 * (line - k)) if k else (0,)
        for y in range(2):
            slots.append(tuple(i + y * len(holders) for i in slot))
            place += [at >= k, 2 * ((at - k) % line) + (side + y) % 2]
    place = jnp.stack([jnp.asarray(value, jnp.int32) for value in place + [core]])
    half, back = line // 2, line - 1
    groups = ([0], [back], [1, half])
    group_places = [
        jnp.stack([(at - k) % line for k in group] + [side]).astype(jnp.int32) for group in groups
    ]
    index = dict(
        own_sect=sect,
        other_sect=1 - sect,
        own_side=side * chip_width,
        other_side=(1 - side) * chip_width,
        upper=at >= half,
        near_core=core == 0,
        share=lax.axis_index("tp"),
        columns=[(at + k) % line * 2 * chip_width for k in shifts],
    )
    length, partial, blocks = heads.shape[1] // 2, None, []
    for part in range(2):
        own = heads[:, part * length : (part + 1) * length]
        if part:
            own, weight, residual_rows, place, group_places, index = lax.optimization_barrier(
                (own, weight, residual_rows, place, group_places, index)
            )
        rights, lefts = [own], [own]
        for k in shifts[1:]:
            if k == 3 and not part:
                rights[-1], sibling_proj = lax.optimization_barrier((rights[-1], sibling_proj))
            right = [(i, i + 1) for i in range(k - 1, line - 1)]
            left = [(i, i - 1) for i in range(1, line - k + 1)]
            rights.append(lax.ppermute(rights[-1], "line", right))
            lefts.append(lax.ppermute(lefts[-1], "line", left))
        near = [own] + [value for pair in zip(rights[1:], lefts[1:]) for value in pair]
        far = [
            lax.ppermute(
                value, ("line", "side"), [(2 * i + y, 2 * i + 1 - y) for i in held for y in range(2)]
            )
            for value, held in zip(near, holders)
        ]
        blocks.append(near + far)
    for part in range(2):
        partial = project(
            place,
            slots,
            blocks[part],
            own_proj,
            sibling_proj,
            part * length,
            partial,
            BF16 if part and tp == 1 else F32,
        )
    if tp > 1:
        partial = lax.psum(partial, "tp").astype(BF16)
    partial = partial.reshape(2, -1, chip_width)
    kept = part_of(partial, index["own_sect"], 1, 0)[0]
    given = part_of(partial, index["other_sect"], 1, 0)[0]
    attention = kept.astype(F32) + swap(given, "sect").astype(F32)
    own_rows = (residual_rows.astype(F32) + attention).astype(BF16)

    got = {k: shift(own_rows, k) if k else own_rows for k in shifts if k != line // 2}
    right = lax.ppermute(got[1], "line", [(i, i + 1) for i in range(1, line - 1)])
    left = lax.ppermute(got[line - 1], "line", [(i, i - 1) for i in range(1, line - 1)])
    got[line // 2] = jnp.where(index["upper"], right, left)
    pairs, opposites = {}, {}
    for k in (0, back, 1, half):
        first, second = ("sect", "side") if k % 2 == 0 else ("side", "sect")
        pairs[k] = jnp.stack([got[k], swap(got[k], first)])
        opposites[k] = swap(pairs[k], second)
    layout = [
        [[(0, 0), (1, 0)], [(0, 1), (1, 1)]] if k % 2 == 0 else [[(0, 0), (0, 1)], [(1, 0), (1, 1)]]
        for k in shifts
    ]
    sums = None
    for group, places in zip(groups, group_places):
        if group == [back]:
            for k in (back, 1, half):
                opposites[k], _ = lax.optimization_barrier((opposites[k], sums))
        sums = hidden_part(
            [layout[k] for k in group],
            places,
            [
                piece
                for k in group
                for piece in (
                    pairs[k], opposites[k], swap(pairs[k], "core"), swap(opposites[k], "core")
                )
            ],
            w_gate[0],
            w_up[0],
            sums,
            weight if half in group else None,
        )
    hidden = sums

    def own_side(value):
        return part_of(value, index["own_side"], chip_width, value.ndim - 1)

    def other_side(value):
        return part_of(value, index["other_side"], chip_width, value.ndim - 1)

    count = row_total // 2
    send, keep = (
        jnp.dot(rows, w_down[0], preferred_element_type=F32) for rows in (hidden[count:], hidden[:count])
    )
    if tp > 1:
        send, keep = (lax.psum(v, "tp") for v in (send, keep))
    send, keep = send.astype(BF16), keep.astype(BF16)

    def columns_to(value, k):
        return part_of(value, index["columns"][k], 2 * chip_width, 1)

    total, held = own_rows.astype(F32), None
    for group in ((half, 1), (back, 0)):
        arrived = swap(jnp.stack([columns_to(send, k) for k in group]), "core")
        if held is not None:
            arrived, held = lax.optimization_barrier((arrived, held))
        for k, arrival in zip(group, arrived):
            part = add(columns_to(keep, k), arrival).reshape(2, -1, 2 * chip_width)
            if k % 2 == 0:
                part = add(part[0], swap(part[1], "sect"))
                held = part
                part = add(own_side(part), swap(other_side(part), "side"))
            else:
                part = add(own_side(part), swap(other_side(part), "side"))
                part = add(part[0], swap(part[1], "sect"))
            total = total + (shift(part, k) if k else part).astype(F32)
    total = total.astype(BF16)

    mine = jnp.where(index["near_core"], total[:, :width], total[:, width:])
    other = swap(jnp.where(index["near_core"], total[:, width:], total[:, :width]), "core")
    out = jnp.where(index["near_core"], jnp.stack([mine, other]), jnp.stack([other, mine]))
    out = out.reshape(2, -1, block, width).transpose(1, 0, 2, 3).reshape(-1, width)
    share = out.shape[0] // tp
    return part_of(out, index["share"] * share, share, 0) if tp > 1 else out


def solution(mesh):
    sizes = dict(mesh.shape)
    fine = Mesh(
        mesh.devices.reshape(sizes["sect"], sizes["grp"] // 4, 2, 2, sizes["tp"]),
        ("sect", "line", "side", "core", "tp"),
    )
    return jax.shard_map(
        on_device,
        mesh=fine,
        in_specs=(
            P(GRP, HID, None),
            P(GRP, None, None),
            P(GRP),
            P(HID, None, None),
            P(HID, GRP),
            P(None, GRP),
            P(GRP, None, HID),
            P(GRP, None, HID),
            P(GRP, HID, None),
            P(),
            P(),
        ),
        out_specs=P(HID, GRP),
        check_vma=False,
    )
```
